256 devices in a mesh: loop: 8 (over y, x_hi), fsdp: 32 (over x_lo, z, core).
Axes of the slice: x: 4 (x_hi: 2, x_lo: 2; x = x_hi * 2 + x_lo), y: 4, z: 8, core: 2. Of those that a mesh axis runs over, the one named last changes fastest.
Arguments:
- image_feats: bfloat16 [65536, 1792], P(('loop', 'fsdp')), may hold values from -6 to 6
- text_emb: bfloat16 [65536, 1152], P(('loop', 'fsdp')), may hold values from -6 to 6
- ln_gain: float32 [1792], replicated, may hold values from 0.5 to 1.5
- proj_weight: bfloat16 [1792, 1152], P('fsdp'), may hold values from -0.125 to 0.125
- log_temp: float32 [1], replicated, may hold values from 2.3 to 3.4
- bias: float32 [1], replicated, may hold values from -4 to -2
Outputs:
- image_grad: bfloat16 [65536, 1792], P(('loop', 'fsdp'))
- text_grad: bfloat16 [65536, 1152], P(('loop', 'fsdp'))
- weight_grad: float32 [1792, 1152], P('fsdp')
- gain_grad: float32 [1792], replicated
The draws below stay inside these ranges and needn't reach their ends.
All inputs are finite; a program needn't handle non-finite values.
Results may differ from the reference program's by a relative error of at most 0.0075.
Values may be sent and summed in bfloat16 or wider, within the bound.
No kernel may reach another device: no remote copies, remote signals or barrier semaphores. Data moves between devices by JAX's collectives and lax.ppermute only.
A program may use at most 128 MiB of HBM per device.

```python
import jax
import jax.numpy as jnp
from jax import lax

D = 1792
E = 1152
TOK_DEV = 256
GROUP = 2048
TOKENS = 65536
N_LOOP = 8
N_FSDP = 32


def level_of(rng, shape, pieces, smallest, top_value):
    gain = 1.0
    for position, parts in pieces:
        draws = jax.random.uniform(jax.random.fold_in(jax.random.fold_in(rng, 6), position), (parts,), jnp.float32, smallest / len(pieces), top_value / len(pieces))
        gain = gain * jnp.repeat(jnp.exp(draws), shape[position] // parts).reshape((-1,) + (1,) * (len(shape) - 1 - position))
    return gain


def normal_values(own_key, dims, scale, bound, cuts=(), kind=jnp.bfloat16):
    loudness = level_of(own_key, dims, cuts, -0.22, 0.18) if cuts else 1.0
    values = jax.random.normal(own_key, dims, jnp.float32) * scale * loudness
    return jnp.minimum(jnp.maximum(values, -bound), bound).astype(kind)


def setup_inputs(seed: int = 0) -> dict:
    keys = jax.random.split(jax.random.key(seed), 7)
    return {
        "image_feats": normal_values(keys[0], (TOKENS, D), 1.0, 6.0, ((0, 256),)),
        "text_emb": normal_values(keys[1], (TOKENS, E), 1.0, 6.0, ((0, 256),)),
        "ln_gain": jnp.clip(1.0 + 0.1 * jax.random.normal(keys[2], (D,), jnp.float32), 0.5, 1.5),
        "proj_weight": normal_values(keys[3], (D, E), D ** -0.5, 0.125, ((0, 32),)),
        "log_temp": jnp.clip(jax.random.uniform(keys[4], (1,), jnp.float32, 2.3, 3.4), 2.3, 3.4),
        "bias": jnp.clip(jax.random.uniform(keys[5], (1,), jnp.float32, -4.0, -2.0), -4.0, -2.0),
    }


def reference(image_feats, text_emb, ln_gain, proj_weight, log_temp, bias):
    feats = image_feats.astype(jnp.float32)
    centered = feats - lax.optimization_barrier(jnp.mean(feats, -1, keepdims=True))
    inv_std = lax.rsqrt(lax.optimization_barrier(jnp.mean(centered * centered, -1, keepdims=True)) + 1e-06)
    normed = centered * inv_std
    hidden = (normed * ln_gain).astype(jnp.bfloat16)
    projected = jnp.dot(hidden, proj_weight, preferred_element_type=jnp.float32)
    image_norm = jnp.sqrt(lax.optimization_barrier(jnp.sum(projected * projected, -1, keepdims=True)) + 1e-06)
    image_unit = projected / image_norm
    image_bf = image_unit.astype(jnp.bfloat16)
    text_f = text_emb.astype(jnp.float32)
    text_norm = jnp.sqrt(lax.optimization_barrier(jnp.sum(text_f * text_f, -1, keepdims=True)) + 1e-06)
    text_unit = text_f / text_norm
    text_bf = text_unit.astype(jnp.bfloat16)
    temper = jnp.exp(log_temp[0])
    offset = bias[0]
    width = image_bf.shape[1]
    image_groups = image_bf.reshape(N_LOOP, N_FSDP, TOK_DEV, width).transpose(1, 0, 2, 3).reshape(N_FSDP, GROUP, width)
    text_groups = text_bf.reshape(N_LOOP, N_FSDP, TOK_DEV, width).transpose(1, 0, 2, 3).reshape(N_FSDP, GROUP, width)

    def one_group(pair):
        images, texts = pair
        logits = temper * lax.dot_general(images, texts, (((1,), (1,)), ((), ())), preferred_element_type=jnp.float32) + offset
        rows_id = lax.broadcasted_iota(jnp.int32, logits.shape, 0)
        cols_id = lax.broadcasted_iota(jnp.int32, logits.shape, 1)
        signs = jnp.where(rows_id == cols_id, 1.0, -1.0).astype(jnp.float32)
        slopes = -signs * jax.nn.sigmoid(-signs * logits)
        slopes_bf = slopes.astype(jnp.bfloat16)
        unit_grad = temper * jnp.dot(slopes_bf, texts, preferred_element_type=jnp.float32)
        text_accum = temper * lax.dot_general(slopes_bf, images, (((0,), (0,)), ((), ())), preferred_element_type=jnp.float32)
        return (unit_grad, text_accum)
    unit_grad, text_accum = lax.map(one_group, (image_groups, text_groups))
    unit_grad = unit_grad.reshape(N_FSDP, N_LOOP, TOK_DEV, width).transpose(1, 0, 2, 3).reshape(TOKENS, width)
    text_accum = text_accum.reshape(N_FSDP, N_LOOP, TOK_DEV, width).transpose(1, 0, 2, 3).reshape(TOKENS, width)
    along = lax.optimization_barrier(jnp.sum(image_unit * unit_grad, -1, keepdims=True))
    proj_grad = ((unit_grad - image_unit * along) / image_norm).astype(jnp.bfloat16)
    weight_grad = lax.dot_general(hidden, proj_grad, (((0,), (0,)), ((), ())), preferred_element_type=jnp.float32)
    hidden_grad = lax.dot_general(proj_grad, proj_weight, (((1,), (1,)), ((), ())), preferred_element_type=jnp.float32)
    gain_grad = lax.optimization_barrier(jnp.sum(hidden_grad * normed, 0))
    back = hidden_grad * ln_gain
    image_grad = (inv_std * (back - lax.optimization_barrier(jnp.mean(back, -1, keepdims=True)) - normed * lax.optimization_barrier(jnp.mean(back * normed, -1, keepdims=True)))).astype(jnp.bfloat16)
    text_along = lax.optimization_barrier(jnp.sum(text_unit * text_accum, -1, keepdims=True))
    text_grad = ((text_accum - text_unit * text_along) / text_norm).astype(jnp.bfloat16)
    return (image_grad, text_grad, weight_grad, gain_grad)
```

```python
import jax
import jax.numpy as jnp
from jax import lax
from jax.sharding import Mesh, PartitionSpec as P

AXES = ("y", "xh", "xl", "z", "c")
LOOP = ("y", "xh")
FSDP = ("xl", "z", "c")
BF = jnp.bfloat16
F32 = jnp.float32
PART_A = 144
COLS_A = 640


def moved(value, axis, by):
    devices = lax.axis_size(axis)
    return lax.ppermute(value, axis, [(i, (i + by) % devices) for i in range(devices)])


def around(value, axis):
    return [moved(value, axis, -k) for k in (1, 2, 3)]


def gathered_weight(shard):
    xl, z, c = lax.axis_index("xl"), lax.axis_index("z"), lax.axis_index("c")
    rows, width = shard.shape
    other = moved(shard, "xl", 1)
    pair = jnp.where(xl == 0, jnp.stack([shard, other]), jnp.stack([other, shard]))
    whole = jnp.zeros((2, 8, 2, rows, width), shard.dtype)

    def put(whole, block, place, core):
        return lax.dynamic_update_slice(whole, block[:, None, None], (0, place % 8, core, 0, 0))

    right, left = pair, pair
    whole = put(whole, pair, z, c)
    whole = put(whole, moved(pair, "c", 1), z, 1 - c)
    for step in range(1, 4):
        right, left = moved(right, "z", 1), moved(left, "z", -1)
        whole = put(whole, right, z - step + 8, c)
        whole = put(whole, left, z + step, c)
        both = moved(jnp.concatenate([right, left]), "c", 1)
        whole = put(whole, both[:2], z - step + 8, 1 - c)
        whole = put(whole, both[2:], z + step, 1 - c)
    last = jnp.concatenate([moved(right[:1], "z", 1), moved(left[1:], "z", -1)])
    whole = put(whole, last, z + 4, c)
    whole = put(whole, moved(last, "c", 1), z + 4, 1 - c)
    return whole.reshape(64 * rows // 2, width)


def slopes_for(image_bf, block, positive, temper, offset):
    logits = (
        temper
        * lax.dot_general(
            image_bf, block, (((1,), (1,)), ((), ())), preferred_element_type=F32
        )
        + offset
    )
    if positive is None:
        return jax.nn.sigmoid(logits).astype(BF)
    signs = jnp.where(positive, 1.0, -1.0).astype(F32)
    return (-signs * jax.nn.sigmoid(-signs * logits)).astype(BF)


def rows_of(core, y, x):
    index = lax.broadcasted_iota(jnp.int32, (1024, 1), 0)
    to_y = (y + index // 256) % 4
    to_x = (x + index // 64 % 4) % 4
    z = index // 8 % 8
    row = index % 8
    shard = to_x % 2 * 16 + z * 2 + core
    found = shard * 56 + (to_y * 2 + to_x // 2) * 7 + row
    return jnp.where(row < 7, found, -1)


def picked(hidden, core, y, x):
    ids = lax.broadcasted_iota(jnp.int32, (1024, hidden.shape[1]), 1)
    choose = (rows_of(core, y, x) == ids).astype(BF)
    return lax.dot_general(
        choose, hidden, (((1,), (1,)), ((), ())), preferred_element_type=F32
    ).astype(BF)


def scattered(own, parts, axis):
    total = own
    for k, part in zip((1, 2, 3), parts):
        total = total + moved(part.astype(BF), axis, k).astype(F32)
    return total


def body(image_feats, text_emb, ln_gain, proj_weight, log_temp, bias):
    rows = image_feats.shape[0]
    y, c = lax.axis_index("y"), lax.axis_index("c")
    x = lax.axis_index(("xh", "xl"))
    full_weight = gathered_weight(proj_weight)

    text_f = text_emb.astype(F32)
    text_norm = jnp.sqrt(jnp.sum(text_f * text_f, -1, keepdims=True) + 1e-06)
    text_unit = text_f / text_norm
    text_bf = text_unit.astype(BF)
    text_a, text_b = text_bf[:PART_A], text_bf[PART_A:]
    both_a = jnp.stack([text_a, moved(text_a, "xh", 1)])
    all_b = jnp.stack([text_b] + around(text_b, "y"))
    all_a = jnp.stack([both_a] + around(both_a, "y"))
    peer_b = moved(all_b, "xh", 1)
    near = jnp.concatenate([all_a[:, 0], all_b], 1).reshape(4 * rows, -1)
    far = jnp.concatenate([all_a[:, 1], peer_b], 1).reshape(4 * rows, -1)
    texts = jnp.concatenate([near, far])

    feats = image_feats.astype(F32)
    centered = feats - jnp.mean(feats, -1, keepdims=True)
    inv_std = lax.rsqrt(jnp.mean(centered * centered, -1, keepdims=True) + 1e-06)
    normed = centered * inv_std
    hidden = (normed * ln_gain).astype(BF)
    mine = picked(hidden, c, y, x)
    theirs = moved(picked(hidden, 1 - c, y, x), "c", 1)
    turned = jnp.concatenate([mine, theirs], 1)
    turned_a = turned.reshape(4, 256, 512)
    turned_b = turned.reshape(4, 4, 64, 512).transpose(1, 0, 2, 3).reshape(4, 256, 512)

    projected = jnp.dot(hidden, full_weight, preferred_element_type=F32)
    image_norm = jnp.sqrt(jnp.sum(projected * projected, -1, keepdims=True) + 1e-06)
    image_unit = projected / image_norm
    image_bf = image_unit.astype(BF)
    image_peer = moved(image_bf, "xh", 1)
    temper = jnp.exp(log_temp[0])
    offset = bias[0]
    row_ids = lax.broadcasted_iota(jnp.int32, (rows, 8 * rows), 0)
    col_ids = lax.broadcasted_iota(jnp.int32, (rows, 8 * rows), 1)
    slopes = slopes_for(image_bf, texts, row_ids == col_ids, temper, offset)
    unit_grad = temper * jnp.dot(slopes, texts, preferred_element_type=F32)
    along = jnp.sum(image_unit * unit_grad, -1, keepdims=True)
    proj_grad = ((unit_grad - image_unit * along) / image_norm).astype(BF)
    both_grad = jnp.concatenate([proj_grad, moved(proj_grad, "c", 1)])

    def weight_part(turned, k, left, right):
        return jnp.dot(turned[k], both_grad[:, left:right], preferred_element_type=F32)

    split, width = COLS_A, proj_grad.shape[1]
    sum_a = scattered(
        weight_part(turned_a, 0, 0, split),
        [weight_part(turned_a, k, 0, split) for k in (1, 2, 3)],
        "y",
    )
    sum_b = scattered(
        weight_part(turned_b, 0, split, width),
        [weight_part(turned_b, k, split, width) for k in (1, 2, 3)],
        ("xh", "xl"),
    )
    sum_a, sum_b = sum_a.reshape(4, 64, split), sum_b.reshape(4, 64, width - split)
    sum_a = scattered(sum_a[0], sum_a[1:], ("xh", "xl"))
    sum_b = scattered(sum_b[0], sum_b[1:], "y")
    piece = jnp.concatenate([sum_a, sum_b], 1).astype(BF).reshape(8, 8, width)
    piece = jnp.sum(lax.all_to_all(piece, "z", 0, 0, tiled=True).astype(F32), 0)
    pieces = lax.all_to_all(jnp.broadcast_to(piece, (8, 8, width)), LOOP, 0, 0, tiled=True)
    weight_grad = pieces[:, :7].reshape(56, width)

    hidden_grad = lax.dot_general(
        proj_grad, full_weight, (((1,), (1,)), ((), ())), preferred_element_type=F32
    )
    gain_part = jnp.sum(hidden_grad * normed, 0)
    gain_part = jnp.pad(gain_part, (0, 256)).reshape(16, 128)
    for axes, many in ((LOOP, 8), (FSDP, 32)):
        gain_part = jnp.sum(
            lax.all_to_all(jnp.broadcast_to(gain_part, (many, 16, 128)), axes, 0, 0, tiled=True), 0
        )
    gain_grad = gain_part.reshape(2048)[:1792]
    back = hidden_grad * ln_gain
    image_grad = (
        inv_std
        * (
            back
            - jnp.mean(back, -1, keepdims=True)
            - normed * jnp.mean(back * normed, -1, keepdims=True)
        )
    ).astype(BF)

    peer_slopes = slopes_for(image_peer, near, None, temper, offset)

    def text_part(k):
        cut = slice(k * rows, (k + 1) * rows)
        turn = (((0,), (0,)), ((), ()))
        return temper * (
            lax.dot_general(slopes[:, cut], image_bf, turn, preferred_element_type=F32)
            + lax.dot_general(peer_slopes[:, cut], image_peer, turn, preferred_element_type=F32)
        )

    text_accum = scattered(text_part(0), [text_part(k) for k in (1, 2, 3)], "y")
    text_along = jnp.sum(text_unit * text_accum, -1, keepdims=True)
    text_grad = ((text_accum - text_unit * text_along) / text_norm).astype(BF)
    return (image_grad, text_grad, weight_grad, gain_grad)


def solution(mesh):
    fine = Mesh(mesh.devices.reshape(4, 2, 2, 8, 2), AXES)
    whole = P(AXES, None)
    in_specs = (whole, whole, P(), P(FSDP, None), P(), P())
    out_specs = (whole, whole, P(FSDP, None), P())
    return jax.shard_map(body, mesh=fine, in_specs=in_specs, out_specs=out_specs, check_vma=False)
```

```python
import jax
import jax.numpy as jnp
from jax import lax
from jax.experimental import pallas as pl
from jax.experimental.pallas import tpu as pltpu
from jax.sharding import Mesh, PartitionSpec as P

AXES = ("y", "xh", "xl", "z", "c")
FSDP = ("xl", "z", "c")
ROW = ("xh", "xl")
BF = jnp.bfloat16
F32 = jnp.float32
VMEM_BYTES = 40 * 1024 * 1024
LAST = (((1,), (1,)), ((), ()))


def moved(value, axis, by):
    devices = lax.axis_size(axis)
    return lax.ppermute(value, axis, [(i, (i + by) % devices) for i in range(devices)])


def around(value, axis):
    return [moved(value, axis, -k) for k in (1, 2, 3)]


def after(value, *others):
    return lax.optimization_barrier((value, others))[0]


def swapped(value, axis, bit):
    devices = lax.axis_size(axis)
    return lax.ppermute(value, axis, [(i, i ^ bit) for i in range(devices)])


def in_three(vector):
    high = lax.reduce_precision(vector, 8, 7)
    middle = lax.reduce_precision(vector - high, 8, 7)
    return jnp.stack([high, middle, vector - high - middle]).astype(BF)


def weight_row(place, core, xl, z):
    core = (core + place // 896) % 2
    xl = (xl + place // 448 % 2) % 2
    block = place // 56 % 8
    away = (block + 1) // 2
    z = (z + jnp.where(block % 2 == 1, 8 - away, away)) % 8
    return (xl * 16 + z * 2 + core) * 56 + place % 56


def picked_row(index, core, y):
    shard = index // 128 % 2 * 16 + index // 16 % 8 * 2 + core
    found = shard * 56 + (y + index // 256) % 4 * 14 + index % 16
    return jnp.where(index % 16 < 14, found, -1)


def slopes_of(scalars, left, right, own):
    dots = lax.dot_general(left, right, LAST, preferred_element_type=F32)
    logits = scalars[0] * dots + scalars[1]
    if own:
        row_ids = lax.broadcasted_iota(jnp.int32, logits.shape, 0)
        col_ids = lax.broadcasted_iota(jnp.int32, logits.shape, 1)
        signs = jnp.where(row_ids == col_ids, 1.0, -1.0).astype(F32)
        slopes = -signs * jax.nn.sigmoid(-signs * logits)
    else:
        slopes = jax.nn.sigmoid(logits)
    return slopes.astype(BF)


def image_kernel(scalars, image_bf, image_unit, image_norm, *refs):
    texts, out = refs[:8], refs[8]
    images = image_bf[...]
    total = jnp.zeros(image_unit.shape, F32)
    for k in range(8):
        block = texts[k][...]
        slopes = slopes_of(scalars, images, block, k == 0)
        total = total + jnp.dot(slopes, block, preferred_element_type=F32)
    total = scalars[0] * total
    unit = image_unit[...]
    along = jnp.sum(unit * total, -1, keepdims=True)
    out[...] = ((total - unit * along) / image_norm[...]).astype(BF)


def text_kernel(scalars, image_own, image_peer, *refs):
    texts, outs = refs[:4], refs[4:]
    own, peer = image_own[...], image_peer[...]
    for k in range(4):
        block = texts[k][...]
        part = jnp.dot(slopes_of(scalars, block, own, k == 0), own, preferred_element_type=F32)
        part = part + jnp.dot(
            slopes_of(scalars, block, peer, False), peer, preferred_element_type=F32
        )
        outs[k][...] = (scalars[0] * part).astype(outs[k].dtype)


def local_call(kernel, outs, inputs):
    scalar = pl.BlockSpec(memory_space=pltpu.SMEM)
    return pl.pallas_call(
        kernel,
        out_shape=outs,
        in_specs=[scalar] + [pl.BlockSpec(memory_space=pltpu.VMEM)] * (len(inputs) - 1),
        out_specs=[pl.BlockSpec(memory_space=pltpu.VMEM)] * len(outs),
        compiler_params=pltpu.CompilerParams(vmem_limit_bytes=VMEM_BYTES),
        cost_estimate=pl.CostEstimate(
            flops=16 * 2 * 256 * 256 * 1152, bytes_accessed=8 * 1024 * 1024, transcendentals=2**19
        ),
    )(*inputs)


def body(image_feats, text_emb, ln_gain, proj_weight, log_temp, bias):
    rows, feat_width = image_feats.shape
    width = proj_weight.shape[1]
    half = feat_width // 2
    y, xl, z, c = (lax.axis_index(name) for name in ("y", "xl", "z", "c"))
    scalars = jnp.stack([jnp.exp(log_temp[0]), bias[0]])

    near_z = [moved(proj_weight, "z", by) for by in (1, -1, 2, -2)]
    text_f = text_emb.astype(F32)
    text_norm = jnp.sqrt(jnp.sum(text_f * text_f, -1, keepdims=True) + 1e-06)
    text_unit = text_f / text_norm
    text_bf = text_unit.astype(BF)
    text_peer = moved(text_bf, "xh", 1)
    near = [text_bf] + around(text_bf, "y")

    down_1, up_1, down_2, up_2 = after(near_z, text_bf)
    below = moved(jnp.concatenate([down_1, down_2[:32]]), "z", 2)
    above = moved(jnp.concatenate([up_1, up_2[32:]]), "z", -2)
    far = [text_peer] + around(after(text_peer, down_1), "y")

    place = lax.broadcasted_iota(jnp.int32, (feat_width, feat_width), 1)
    name = lax.broadcasted_iota(jnp.int32, (feat_width, feat_width), 0)
    order = weight_row(place, after(c, text_peer), xl, z) == name
    order_bf = order.astype(BF)
    feats = jnp.dot(after(image_feats, text_peer), order_bf, preferred_element_type=F32)
    gain = jnp.sum(jnp.dot(in_three(ln_gain), order_bf, preferred_element_type=F32), 0)
    centered = feats - jnp.mean(feats, -1, keepdims=True)
    inv_std = lax.rsqrt(jnp.mean(centered * centered, -1, keepdims=True) + 1e-06)
    normed = centered * inv_std
    hidden = (normed * gain).astype(BF)

    below, above = after((below, above), text_peer)
    shards = [proj_weight, down_1, up_1, down_2, up_2, below[:56], above[:56]]
    shards = jnp.concatenate(shards + [below[56:], above[56:]])
    quarter = shards.shape[0] // 2
    others = [moved(shards[:quarter], ROW, 1), moved(shards[quarter:], ROW, -1)]
    weight_mine = jnp.concatenate([shards] + after(others, hidden, near))
    weight_other = moved(weight_mine, "c", 1)

    weight_place = weight_row(lax.broadcasted_iota(jnp.int32, (1, feat_width), 1), c, xl, z)
    wanted = lax.broadcasted_iota(jnp.int32, (1024, 1), 0)
    late_hidden = after(hidden, weight_mine)

    def picked(core):
        choose = (picked_row(wanted, core, y) == weight_place).astype(BF)
        return lax.dot_general(choose, late_hidden, LAST, preferred_element_type=F32).astype(BF)

    theirs = moved(picked(1 - c), "c", 1)
    mine = picked(c)

    weight_other = after(weight_other, mine, far)
    projected = jnp.dot(hidden[:, :half], weight_mine, preferred_element_type=F32) + jnp.dot(
        hidden[:, half:], weight_other, preferred_element_type=F32
    )
    image_norm = jnp.sqrt(jnp.sum(projected * projected, -1, keepdims=True) + 1e-06)
    image_unit = projected / image_norm
    image_bf = image_unit.astype(BF)
    image_peer = moved(image_bf, "xh", 1)

    (proj_grad,) = local_call(
        image_kernel,
        [jax.ShapeDtypeStruct((rows, width), BF)],
        [scalars, image_bf, image_unit, image_norm] + near + far,
    )
    both_grad = jnp.concatenate([proj_grad, moved(proj_grad, "c", 1)])
    turned = jnp.concatenate([mine, theirs], 1).reshape(4, rows, 2 * rows)

    hidden_grad = jnp.concatenate(
        [
            lax.dot_general(proj_grad, weight_mine, LAST, preferred_element_type=F32),
            lax.dot_general(proj_grad, weight_other, LAST, preferred_element_type=F32),
        ],
        1,
    )
    gain_part = jnp.sum(hidden_grad * normed, 0)


    parts = [jnp.dot(turned[k], both_grad, preferred_element_type=F32) for k in (1, 2, 3, 0)]
    sends = [part.astype(BF) for part in parts[:3]]
    total = parts[3]
    arrived = [moved(sends[k - 1], "y", k) for k in (1, 2, 3)]

    text_parts = local_call(
        text_kernel,
        [jax.ShapeDtypeStruct((rows, width), F32 if k == 0 else BF) for k in range(4)],
        [after(scalars, sends), image_bf, image_peer] + near,
    )
    gain_parts = lax.dot_general(
        in_three(after(gain_part, sends)), order_bf, LAST, preferred_element_type=F32
    )
    gain_part = jnp.pad(jnp.sum(gain_parts, 0), (0, 256)).reshape(16, 128)
    gain_part = jnp.broadcast_to(gain_part, (32, 16, 128))
    gain_part = jnp.sum(lax.all_to_all(gain_part, FSDP, 0, 0, tiled=True), 0)

    arrived = after(arrived, text_parts, gain_part)
    for part in arrived:
        total = total + part.astype(F32)
    total = total.astype(BF).reshape(16, 16, width)
    shared = lax.all_to_all(total, ("xl", "z"), 0, 0, tiled=True)

    gain_part = after(gain_part, total)
    gain_part = gain_part + swapped(gain_part, "xh", 1)
    text_sends = after(text_parts[1:], total)
    text_arrived = [moved(text_sends[k - 1], "y", k) for k in (1, 2, 3)]
    back = after(hidden_grad, total) * gain
    image_grad = (
        inv_std
        * (
            back
            - jnp.mean(back, -1, keepdims=True)
            - normed * jnp.mean(back * normed, -1, keepdims=True)
        )
    ).astype(BF)
    image_grad = lax.dot_general(image_grad, order_bf, LAST, preferred_element_type=F32).astype(BF)

    piece = jnp.sum(after(shared, image_grad).astype(F32), 0)
    piece = piece + swapped(piece, "xh", 1)
    gain_part = gain_part + swapped(after(gain_part, shared), "y", 1)
    pieces = jnp.stack([piece] + around(piece, "y"))
    gain_part = gain_part + swapped(after(gain_part, piece), "y", 2)
    pieces = lax.dynamic_slice_in_dim(jnp.concatenate([pieces, pieces]), 4 - y, 4)
    weight_grad = pieces[:, :14].reshape(56, width)
    gain_grad = gain_part.reshape(2048)[:feat_width]

    text_accum = text_parts[0]
    for part in after(text_arrived, pieces):
        text_accum = text_accum + part.astype(F32)
    text_along = jnp.sum(text_unit * text_accum, -1, keepdims=True)
    text_grad = ((text_accum - text_unit * text_along) / text_norm).astype(BF)
    return (image_grad, text_grad, weight_grad, gain_grad)


def solution(mesh):
    fine = Mesh(mesh.devices.reshape(4, 2, 2, 8, 2), AXES)
    whole = P(AXES, None)
    in_specs = (whole, whole, P(), P(FSDP, None), P(), P())
    out_specs = (whole, whole, P(FSDP, None), P())
    return jax.shard_map(body, mesh=fine, in_specs=in_specs, out_specs=out_specs, check_vma=False)
```

```python
import jax
import jax.numpy as jnp
from jax import lax
from jax.experimental import pallas as pl
from jax.experimental.pallas import tpu as pltpu
from jax.sharding import Mesh, PartitionSpec as P

AXES = ("y", "xh", "xl", "z", "c")
FSDP = ("xl", "z", "c")
ROW = ("xh", "xl")
BF = jnp.bfloat16
F32 = jnp.float32
VMEM_BYTES = 18 * 1024 * 1024
LAST = (((1,), (1,)), ((), ()))


def moved(value, axis, by):
    devices = lax.axis_size(axis)
    return lax.ppermute(value, axis, [(i, (i + by) % devices) for i in range(devices)])


def around(value, axis):
    return [moved(value, axis, -k) for k in (1, 2, 3)]


def after(value, *others):
    return lax.optimization_barrier((value, others))[0]


def swapped(value, axis, bit):
    devices = lax.axis_size(axis)
    return lax.ppermute(value, axis, [(i, i ^ bit) for i in range(devices)])


def in_three(vector):
    high = lax.reduce_precision(vector, 8, 7)
    middle = lax.reduce_precision(vector - high, 8, 7)
    return jnp.stack([high, middle, vector - high - middle]).astype(BF)


def weight_row(place, core, xl, z):
    core = (core + place // 896) % 2
    xl = (xl + place // 448 % 2) % 2
    block = place // 56 % 8
    away = (block + 1) // 2
    z = (z + jnp.where(block % 2 == 1, 8 - away, away)) % 8
    return (xl * 16 + z * 2 + core) * 56 + place % 56


def picked_row(index, core, y):
    shard = index // 128 % 2 * 16 + index // 16 % 8 * 2 + core
    found = shard * 56 + (y + index // 256) % 4 * 14 + index % 16
    return jnp.where(index % 16 < 14, found, -1)


def slopes_of(scalars, left, right, own):
    dots = lax.dot_general(left, right, LAST, preferred_element_type=F32)
    logits = scalars[0] * dots + scalars[1]
    if own:
        row_ids = lax.broadcasted_iota(jnp.int32, logits.shape, 0)
        col_ids = lax.broadcasted_iota(jnp.int32, logits.shape, 1)
        signs = jnp.where(row_ids == col_ids, 1.0, -1.0).astype(F32)
        slopes = -signs * jax.nn.sigmoid(-signs * logits)
    else:
        slopes = jax.nn.sigmoid(logits)
    return slopes.astype(BF)


def image_kernel(scalars, image_bf, image_unit, image_norm, *refs):
    texts, out = [ref[...] for ref in refs[:6]] + [refs[6][0], refs[6][1]], refs[7]
    images = image_bf[...]
    total = jnp.zeros(image_unit.shape, F32)
    for k in range(8):
        block = texts[k]
        slopes = slopes_of(scalars, images, block, k == 0)
        total = total + jnp.dot(slopes, block, preferred_element_type=F32)
    total = scalars[0] * total
    unit = image_unit[...]
    along = jnp.sum(unit * total, -1, keepdims=True)
    out[...] = ((total - unit * along) / image_norm[...]).astype(BF)


def text_kernel(scalars, *refs):
    images, texts, outs = refs[:4], refs[4:6], refs[6:]
    for t in (1, 0):
        text = texts[t][...]
        total = jnp.zeros(text.shape, F32)
        for i in range(4):
            image = images[i][...]
            slopes = slopes_of(scalars, text, image, t == 0 and i == 0)
            total = total + jnp.dot(slopes, image, preferred_element_type=F32)
        outs[t][...] = (scalars[0] * total).astype(outs[t].dtype)


def local_call(kernel, outs, inputs):
    scalar = pl.BlockSpec(memory_space=pltpu.SMEM)
    return pl.pallas_call(
        kernel,
        out_shape=outs,
        in_specs=[scalar] + [pl.BlockSpec(memory_space=pltpu.VMEM)] * (len(inputs) - 1),
        out_specs=[pl.BlockSpec(memory_space=pltpu.VMEM)] * len(outs),
        compiler_params=pltpu.CompilerParams(vmem_limit_bytes=VMEM_BYTES),
        cost_estimate=pl.CostEstimate(
            flops=16 * 2 * 256 * 256 * 1152, bytes_accessed=8 * 1024 * 1024, transcendentals=2**19
        ),
    )(*inputs)


def body(image_feats, text_emb, ln_gain, proj_weight, log_temp, bias):
    rows, feat_width = image_feats.shape
    width = proj_weight.shape[1]
    half = feat_width // 2
    y, xl, z, c = (lax.axis_index(name) for name in ("y", "xl", "z", "c"))
    scalars = jnp.stack([jnp.exp(log_temp[0]), bias[0]])

    near_z = [moved(proj_weight, "z", by) for by in (1, -1, 2, -2)]
    text_f = text_emb.astype(F32)
    text_norm = jnp.sqrt(jnp.sum(text_f * text_f, -1, keepdims=True) + 1e-06)
    text_unit = text_f / text_norm
    text_bf = text_unit.astype(BF)

    down_1, up_1, down_2, up_2 = after(near_z, text_bf)
    below = jnp.concatenate([down_1, down_2[:32]])
    above = jnp.concatenate([up_1, up_2[32:]])
    text_bf = after(text_bf, below, above)
    below, above = moved(below, "z", 2), moved(above, "z", -2)
    text_peer = moved(text_bf, "xh", 1)
    first = jnp.concatenate([proj_weight, down_1, up_1, down_2])
    other_first = moved(first, ROW, 1)
    near_up = moved(text_bf, "y", -1)
    second = [up_2, below[:56], above[:56], below[56:], above[56:]]
    second = jnp.concatenate(second)
    other_second = moved(second, ROW, -1)
    near_down = moved(after(text_bf, second), "y", 1)
    far_up, far_down = moved(text_peer, "y", -1), moved(text_peer, "y", 1)
    opposite = moved(after(jnp.stack([text_bf, text_peer]), near_up), "y", 2)
    texts = [text_bf, text_peer, near_up, near_down, far_up, far_down, opposite]

    place = lax.broadcasted_iota(jnp.int32, (feat_width, feat_width), 1)
    name = lax.broadcasted_iota(jnp.int32, (feat_width, feat_width), 0)
    order = weight_row(place, after(c, text_peer, second), xl, z) == name
    order_bf = order.astype(BF)
    feats = jnp.dot(after(image_feats, text_peer, second), order_bf, preferred_element_type=F32)
    gain = jnp.sum(jnp.dot(in_three(ln_gain), order_bf, preferred_element_type=F32), 0)
    centered = feats - jnp.mean(feats, -1, keepdims=True)
    inv_std = lax.rsqrt(jnp.mean(centered * centered, -1, keepdims=True) + 1e-06)
    normed = centered * inv_std
    hidden = (normed * gain).astype(BF)

    others = after([other_first, other_second], hidden, near_up, near_down)
    weight_mine = jnp.concatenate([first, second] + others)
    weight_other = moved(weight_mine, "c", 1)

    weight_place = weight_row(lax.broadcasted_iota(jnp.int32, (1, feat_width), 1), c, xl, z)
    wanted = lax.broadcasted_iota(jnp.int32, (1024, 1), 0)
    late_hidden = after(hidden, weight_mine)

    def picked(core):
        choose = (picked_row(wanted, core, y) == weight_place).astype(BF)
        return lax.dot_general(choose, late_hidden, LAST, preferred_element_type=F32).astype(BF)

    theirs = moved(picked(1 - c), "c", 1)
    mine = picked(c)

    weight_other = after(weight_other, mine, far_up, far_down)
    projected = jnp.dot(hidden[:, :half], weight_mine, preferred_element_type=F32) + jnp.dot(
        hidden[:, half:], weight_other, preferred_element_type=F32
    )
    image_norm = jnp.sqrt(jnp.sum(projected * projected, -1, keepdims=True) + 1e-06)
    image_unit = projected / image_norm
    image_bf = image_unit.astype(BF)
    images = [image_bf] + around(image_bf, "y")

    (proj_grad,) = local_call(
        image_kernel,
        [jax.ShapeDtypeStruct((rows, width), BF)],
        [scalars, image_bf, image_unit, image_norm] + texts,
    )
    both_grad = jnp.concatenate([proj_grad, moved(proj_grad, "c", 1)])
    turned = jnp.concatenate([mine, theirs], 1).reshape(4, rows, 2 * rows)

    hidden_grad = jnp.concatenate(
        [
            lax.dot_general(proj_grad, weight_mine, LAST, preferred_element_type=F32),
            lax.dot_general(proj_grad, weight_other, LAST, preferred_element_type=F32),
        ],
        1,
    )
    gain_part = jnp.sum(hidden_grad * normed, 0)


    parts = [jnp.dot(turned[k], both_grad, preferred_element_type=F32) for k in (1, 2, 3, 0)]
    sends = [part.astype(BF) for part in parts[:3]]
    total = parts[3]
    arrived = [moved(sends[k - 1], "y", k) for k in (1, 2, 3)]

    text_parts = local_call(
        text_kernel,
        [jax.ShapeDtypeStruct((rows, width), kind) for kind in (F32, BF)],
        [after(scalars, sends)] + images + [text_bf, text_peer],
    )
    gain_parts = lax.dot_general(
        in_three(after(gain_part, sends)), order_bf, LAST, preferred_element_type=F32
    )
    text_arrived = moved(text_parts[1], "xh", 1)
    gain_part = jnp.pad(jnp.sum(gain_parts, 0), (0, 256)).reshape(16, 128)
    gain_part = jnp.broadcast_to(gain_part, (32, 16, 128))
    gain_part = jnp.sum(lax.all_to_all(gain_part, FSDP, 0, 0, tiled=True), 0)

    arrived = after(arrived, text_parts, gain_part)
    for part in arrived:
        total = total + part.astype(F32)
    total = total.astype(BF).reshape(16, 16, width)
    shared = lax.all_to_all(total, ("xl", "z"), 0, 0, tiled=True)

    gain_part = after(gain_part, total)
    gain_part = gain_part + swapped(gain_part, "xh", 1)
    back = after(hidden_grad, total) * gain
    image_grad = (
        inv_std
        * (
            back
            - jnp.mean(back, -1, keepdims=True)
            - normed * jnp.mean(back * normed, -1, keepdims=True)
        )
    ).astype(BF)
    image_grad = lax.dot_general(image_grad, order_bf, LAST, preferred_element_type=F32).astype(BF)

    piece = jnp.sum(after(shared, image_grad).astype(F32), 0)
    piece = piece + swapped(piece, "xh", 1)
    gain_part = gain_part + swapped(after(gain_part, shared), "y", 1)
    pieces = jnp.stack([piece] + around(piece, "y"))
    gain_part = gain_part + swapped(after(gain_part, piece), "y", 2)
    pieces = lax.dynamic_slice_in_dim(jnp.concatenate([pieces, pieces]), 4 - y, 4)
    weight_grad = pieces[:, :14].reshape(56, width)
    gain_grad = gain_part.reshape(2048)[:feat_width]

    text_accum = text_parts[0] + text_arrived.astype(F32)
    text_along = jnp.sum(text_unit * text_accum, -1, keepdims=True)
    text_grad = ((text_accum - text_unit * text_along) / text_norm).astype(BF)
    return (image_grad, text_grad, weight_grad, gain_grad)


def solution(mesh):
    fine = Mesh(mesh.devices.reshape(4, 2, 2, 8, 2), AXES)
    whole = P(AXES, None)
    in_specs = (whole, whole, P(), P(FSDP, None), P(), P())
    out_specs = (whole, whole, P(FSDP, None), P())
    return jax.shard_map(body, mesh=fine, in_specs=in_specs, out_specs=out_specs, check_vma=False)
```

```python
import jax
import jax.numpy as jnp
from jax import lax
from jax.experimental import pallas as pl
from jax.experimental.pallas import tpu as pltpu
from jax.sharding import Mesh, PartitionSpec as P

AXES = ("y", "xh", "xl", "z", "c")
FSDP = ("xl", "z", "c")
ROW = ("xh", "xl")
BF = jnp.bfloat16
F32 = jnp.float32
VMEM_BYTES = 24 * 1024 * 1024
LAST = (((1,), (1,)), ((), ()))


def moved(value, axis, by):
    devices = lax.axis_size(axis)
    return lax.ppermute(value, axis, [(i, (i + by) % devices) for i in range(devices)])


def around(value, axis):
    return [moved(value, axis, -k) for k in (1, 2, 3)]


def after(value, *others):
    return lax.optimization_barrier((value, others))[0]


def swapped(value, axis, bit):
    devices = lax.axis_size(axis)
    return lax.ppermute(value, axis, [(i, i ^ bit) for i in range(devices)])


def in_three(vector):
    high = lax.reduce_precision(vector, 8, 7)
    middle = lax.reduce_precision(vector - high, 8, 7)
    return jnp.stack([high, middle, vector - high - middle]).astype(BF)


def weight_row(place, core, xl, z):
    core = (core + place // 896) % 2
    xl = (xl + place // 448 % 2) % 2
    block = place // 56 % 8
    away = (block + 1) // 2
    z = (z + jnp.where(block % 2 == 1, 8 - away, away)) % 8
    return (xl * 16 + z * 2 + core) * 56 + place % 56


def text_unit_of(text):
    wide = text[...].astype(F32)
    norm = jnp.sqrt(jnp.sum(wide * wide, -1, keepdims=True) + 1e-06)
    return wide / norm, norm


def text_unit_kernel(text, out):
    out[...] = text_unit_of(text)[0].astype(BF)


def text_grad_kernel(text, own, arrived, out):
    unit, norm = text_unit_of(text)
    total = own[...] + arrived[...].astype(F32)
    along = jnp.sum(unit * total, -1, keepdims=True)
    out[...] = ((total - unit * along) / norm).astype(BF)


def order_of(place, k):
    rows = lax.broadcasted_iota(jnp.int32, (256, place.shape[1]), 0) + k * 256
    return jnp.where(rows == place, 1.0, 0.0).astype(BF)


def layer_norm_kernel(place_ref, gains, feats, hidden, normed, inv_std, gain):
    place = place_ref[...]
    value = jnp.zeros(feats.shape, F32)
    gain_parts = jnp.zeros(gains.shape, F32)
    for k in range(feats.shape[1] // 256):
        cut = slice(k * 256, (k + 1) * 256)
        order = order_of(place, k)
        value = value + jnp.dot(feats[:, cut], order, preferred_element_type=F32)
        gain_parts = gain_parts + jnp.dot(gains[:, cut], order, preferred_element_type=F32)
    gain_row = jnp.sum(gain_parts, 0, keepdims=True)
    centered = value - jnp.mean(value, -1, keepdims=True)
    scale = lax.rsqrt(jnp.mean(centered * centered, -1, keepdims=True) + 1e-06)
    value = centered * scale
    normed[...] = value
    inv_std[...] = scale
    gain[...] = gain_row
    hidden[...] = (value * gain_row).astype(BF)


def picked_kernel(ids, place_ref, hidden, mine, theirs):
    place = place_ref[...]
    index = lax.broadcasted_iota(jnp.int32, (256, 1), 0)
    inside = index & 15
    for k in range(4):
        for core, out in ((ids[1], mine), (1 - ids[1], theirs)):
            shard = (index >> 7) * 16 + ((index >> 4) & 7) * 2 + core
            found = shard * 56 + ((ids[0] + k) & 3) * 14 + inside
            found = jnp.where(inside < 14, found, -1)
            choose = jnp.where(found == place, 1.0, 0.0).astype(BF)
            part = lax.dot_general(choose, hidden[...], LAST, preferred_element_type=F32)
            out[k * 256 : (k + 1) * 256] = part.astype(BF)


def projection_kernel(hidden, weight_mine, weight_other, image_bf, image_unit, image_norm):
    half = weight_mine.shape[0]
    projected = jnp.dot(hidden[:, :half], weight_mine[...], preferred_element_type=F32)
    projected = projected + jnp.dot(
        hidden[:, half:], weight_other[...], preferred_element_type=F32
    )
    norm = jnp.sqrt(jnp.sum(projected * projected, -1, keepdims=True) + 1e-06)
    unit = projected / norm
    image_norm[...] = norm
    image_unit[...] = unit
    image_bf[...] = unit.astype(BF)


def image_grad_kernel(
    place_ref, proj_grad, weight_mine, weight_other, normed_ref, inv_std, gain, out, gain_out
):
    grad = proj_grad[...]
    hidden_grad = jnp.concatenate(
        [
            lax.dot_general(grad, weight[...], LAST, preferred_element_type=F32)
            for weight in (weight_mine, weight_other)
        ],
        1,
    )
    normed = normed_ref[...]
    gain_part = jnp.sum(hidden_grad * normed, 0, keepdims=True)
    high = gain_part.astype(BF)
    gain_part = gain_part - high.astype(F32)
    middle = gain_part.astype(BF)
    low = (gain_part - middle.astype(F32)).astype(BF)
    back = hidden_grad * gain[...]
    result = (
        inv_std[...]
        * (
            back
            - jnp.mean(back, -1, keepdims=True)
            - normed * jnp.mean(back * normed, -1, keepdims=True)
        )
    ).astype(BF)
    place = place_ref[...]
    for k in range(out.shape[1] // 256):
        cut = slice(k * 256, (k + 1) * 256)
        order = order_of(place, k)
        out[:, cut] = lax.dot_general(result, order, LAST, preferred_element_type=F32).astype(BF)
        total = jnp.zeros((1, 256), F32)
        for part in (high, middle, low):
            total = total + lax.dot_general(part, order, LAST, preferred_element_type=F32)
        gain_out[:, cut] = total


def weight_kernel(mine, theirs, grad_mine, grad_theirs, *refs):
    arrived, out = refs[:-1], refs[-1]
    total = jnp.dot(mine[...], grad_mine[...], preferred_element_type=F32)
    total = total + jnp.dot(theirs[...], grad_theirs[...], preferred_element_type=F32)
    for part in arrived:
        total = total + part[...].astype(F32)
    out[...] = total.astype(BF)


def slopes_of(scalars, left, right, own):
    dots = lax.dot_general(left, right, LAST, preferred_element_type=F32)
    logits = scalars[0] * dots + scalars[1]
    if own:
        row_ids = lax.broadcasted_iota(jnp.int32, logits.shape, 0)
        col_ids = lax.broadcasted_iota(jnp.int32, logits.shape, 1)
        signs = jnp.where(row_ids == col_ids, 1.0, -1.0).astype(F32)
        slopes = -signs * jax.nn.sigmoid(-signs * logits)
    else:
        slopes = jax.nn.sigmoid(logits)
    return slopes.astype(BF)


def image_kernel(scalars, image_bf, image_unit, image_norm, *refs):
    texts, out = refs[:8], refs[8]
    images = image_bf[...]
    total = jnp.zeros(image_unit.shape, F32)
    for k in range(8):
        block = texts[k][...]
        slopes = slopes_of(scalars, images, block, k == 0)
        total = total + jnp.dot(slopes, block, preferred_element_type=F32)
    total = scalars[0] * total
    unit = image_unit[...]
    along = jnp.sum(unit * total, -1, keepdims=True)
    out[...] = ((total - unit * along) / image_norm[...]).astype(BF)


def text_kernel(scalars, *refs):
    images, texts, outs = refs[:4], refs[4:6], refs[6:]
    for t in (1, 0):
        text = texts[t][...]
        total = jnp.zeros(text.shape, F32)
        for i in range(4):
            image = images[i][...]
            slopes = slopes_of(scalars, text, image, t == 0 and i == 0)
            total = total + jnp.dot(slopes, image, preferred_element_type=F32)
        outs[t][...] = (scalars[0] * total).astype(outs[t].dtype)


def local_call(kernel, outs, inputs, scalars=0):
    spaces = [pltpu.SMEM] * scalars + [pltpu.VMEM] * (len(inputs) - scalars)
    results = pl.pallas_call(
        kernel,
        out_shape=[jax.ShapeDtypeStruct(shape, kind) for shape, kind in outs],
        in_specs=[pl.BlockSpec(memory_space=space) for space in spaces],
        out_specs=[pl.BlockSpec(memory_space=pltpu.VMEM)] * len(outs),
        compiler_params=pltpu.CompilerParams(vmem_limit_bytes=VMEM_BYTES),
        cost_estimate=pl.CostEstimate(flops=1, bytes_accessed=1, transcendentals=0),
    )(*inputs)
    return results[0] if len(outs) == 1 else results


def body(image_feats, text_emb, ln_gain, proj_weight, log_temp, bias):
    rows, feat_width = image_feats.shape
    width = proj_weight.shape[1]
    block = (rows, width)
    y, xl, z, c = (lax.axis_index(name) for name in ("y", "xl", "z", "c"))
    scalars = jnp.stack([jnp.exp(log_temp[0]), bias[0]])
    ids = jnp.stack([y, c])
    place = weight_row(lax.broadcasted_iota(jnp.int32, (1, feat_width), 1), c, xl, z)
    gains = jnp.pad(in_three(ln_gain), ((0, 13), (0, 0)))

    near_z = [moved(proj_weight, "z", by) for by in (1, -1, 2, -2)]
    text_bf = local_call(text_unit_kernel, [(block, BF)], [text_emb])
    text_peer = moved(text_bf, "xh", 1)

    down_1, up_1, down_2, up_2 = after(near_z, text_bf)
    below = jnp.concatenate([down_1, down_2[:32]])
    above = jnp.concatenate([up_1, up_2[32:]])
    first = jnp.concatenate([proj_weight, down_1, up_1, down_2])
    text_bf, first = after((text_bf, first), below, above)
    below, above = moved(below, "z", 2), moved(above, "z", -2)
    other_first = moved(first, ROW, 1)
    near = around(text_bf, "y")
    second = [up_2, below[:56], above[:56], below[56:], above[56:]]
    second = jnp.concatenate(second)
    second = after(second, below)
    other_second = moved(second, ROW, -1)
    far = around(text_peer, "y")
    texts = [text_bf, text_peer] + near + far

    hidden, normed, inv_std, gain = local_call(
        layer_norm_kernel,
        [(image_feats.shape, BF), (image_feats.shape, F32), ((rows, 1), F32), ((1, feat_width), F32)],
        [place, gains, after(image_feats, text_peer, second, near)],
    )

    others = after([other_first, other_second], hidden, far)
    weight_mine = jnp.concatenate([first, second] + others)
    weight_other = moved(weight_mine, "c", 1)

    mine, theirs = local_call(
        picked_kernel,
        [((1024, rows), BF)] * 2,
        [ids, place, after(hidden, weight_mine)],
        1,
    )
    theirs = moved(theirs, "c", 1)
    image_bf, image_unit, image_norm = local_call(
        projection_kernel,
        [(block, BF), (block, F32), ((rows, 1), F32)],
        [hidden, weight_mine, after(weight_other, mine)],
    )
    images = [image_bf] + around(image_bf, "y")
    proj_grad = local_call(
        image_kernel,
        [(block, BF)],
        [scalars, image_bf, image_unit, image_norm] + texts,
        1,
    )
    other_grad = moved(proj_grad, "c", 1)

    mine, theirs = mine.reshape(4, rows, rows), theirs.reshape(4, rows, rows)
    sends = [
        local_call(weight_kernel, [(block, BF)], [mine[k], theirs[k], proj_grad, other_grad])
        for k in (1, 2, 3)
    ]
    arrived = [moved(sends[k - 1], "y", k) for k in (1, 2, 3)]

    image_grad, gain_part = local_call(
        image_grad_kernel,
        [(image_feats.shape, BF), ((1, feat_width), F32)],
        [place, after(proj_grad, sends), weight_mine, weight_other, normed, inv_std, gain],
    )

    text_own, text_other = local_call(
        text_kernel,
        [(block, F32), (block, BF)],
        [after(scalars, image_grad)] + images + [text_bf, text_peer],
        1,
    )
    text_arrived = moved(text_other, "xh", 1)
    gain_part = jnp.pad(gain_part[0], (0, 256)).reshape(16, 128)
    gain_part = jnp.broadcast_to(gain_part, (32, 16, 128))
    gain_part = jnp.sum(lax.all_to_all(gain_part, FSDP, 0, 0, tiled=True), 0)

    arrived = after(arrived, text_own, gain_part)
    total = local_call(
        weight_kernel, [(block, BF)], [mine[0], theirs[0], proj_grad, other_grad] + arrived
    )
    shared = lax.all_to_all(total.reshape(16, 16, width), ("xl", "z"), 0, 0, tiled=True)

    gain_part = after(gain_part, total)
    gain_part = gain_part + swapped(gain_part, "xh", 1)
    text_grad = local_call(
        text_grad_kernel, [(block, BF)], [after(text_emb, total), text_own, text_arrived]
    )
    piece = jnp.sum(shared.astype(F32), 0)
    piece = piece + swapped(piece, "xh", 1)
    gain_part = gain_part + swapped(after(gain_part, shared), "y", 1)
    pieces = jnp.stack([piece] + around(piece, "y"))
    gain_part = gain_part + swapped(after(gain_part, piece), "y", 2)
    pieces = lax.dynamic_slice_in_dim(jnp.concatenate([pieces, pieces]), 4 - y, 4)
    weight_grad = pieces[:, :14].reshape(56, width)
    gain_grad = gain_part.reshape(2048)[:feat_width]
    return (image_grad, text_grad, weight_grad, gain_grad)


def solution(mesh):
    fine = Mesh(mesh.devices.reshape(4, 2, 2, 8, 2), AXES)
    whole = P(AXES, None)
    in_specs = (whole, whole, P(), P(FSDP, None), P(), P())
    out_specs = (whole, whole, P(FSDP, None), P())
    return jax.shard_map(body, mesh=fine, in_specs=in_specs, out_specs=out_specs, check_vma=False)
```

```python
import functools

import jax
import jax.numpy as jnp
from jax import lax
from jax.experimental import pallas as pl
from jax.experimental.pallas import tpu as pltpu
from jax.sharding import Mesh, PartitionSpec as P

AXES = ("y", "xh", "xl", "z", "c")
FSDP = ("xl", "z", "c")
ROW = ("xh", "xl")
BF = jnp.bfloat16
F32 = jnp.float32
VMEM_BYTES = 32 * 1024 * 1024
LAST = (((1,), (1,)), ((), ()))


def moved(value, axis, by):
    devices = lax.axis_size(axis)
    return lax.ppermute(value, axis, [(i, (i + by) % devices) for i in range(devices)])


def around(value, axis):
    return [moved(value, axis, -k) for k in (1, 2, 3)]


def after(value, *others):
    return lax.optimization_barrier((value, others))[0]


def swapped(value, axis, bit):
    devices = lax.axis_size(axis)
    return lax.ppermute(value, axis, [(i, i ^ bit) for i in range(devices)])


def in_three(vector):
    high = lax.reduce_precision(vector, 8, 7)
    middle = lax.reduce_precision(vector - high, 8, 7)
    return jnp.stack([high, middle, vector - high - middle]).astype(BF)


def weight_row(place, core, xl, z):
    core = (core + place // 896) % 2
    xl = (xl + place // 448 % 2) % 2
    block = place // 56 % 8
    away = (block + 1) // 2
    z = (z + jnp.where(block % 2 == 1, 8 - away, away)) % 8
    return (xl * 16 + z * 2 + core) * 56 + place % 56


def text_unit_of(text):
    wide = text[...].astype(F32)
    norm = jnp.sqrt(jnp.sum(wide * wide, -1, keepdims=True) + 1e-06)
    return wide / norm, norm


def text_unit_kernel(text, out):
    out[...] = text_unit_of(text)[0].astype(BF)


def text_grad_kernel(text, own, *refs):
    arrived, out = refs[:-1], refs[-1]
    unit, norm = text_unit_of(text)
    total = own[...]
    for part in arrived:
        total = total + part[...].astype(F32)
    along = jnp.sum(unit * total, -1, keepdims=True)
    out[...] = ((total - unit * along) / norm).astype(BF)


def order_of(place, k):
    rows = lax.broadcasted_iota(jnp.int32, (256, place.shape[1]), 0) + k * 256
    return jnp.where(rows == place, 1.0, 0.0).astype(BF)


def layer_norm_kernel(
    place_ref, gains, feats, feats_peer, hidden, normed, inv_std, gain, hidden_peer
):
    place = place_ref[...]
    gain_parts = jnp.zeros(gains.shape, F32)
    for source in (feats, feats_peer):
        value = jnp.zeros(feats.shape, F32)
        for k in range(feats.shape[1] // 256):
            cut = slice(k * 256, (k + 1) * 256)
            order = order_of(place, k)
            value = value + jnp.dot(source[:, cut], order, preferred_element_type=F32)
            if source is feats:
                gain_parts = gain_parts + jnp.dot(
                    gains[:, cut], order, preferred_element_type=F32
                )
        if source is feats:
            gain[...] = jnp.sum(gain_parts, 0, keepdims=True)
        centered = value - jnp.mean(value, -1, keepdims=True)
        scale = lax.rsqrt(jnp.mean(centered * centered, -1, keepdims=True) + 1e-06)
        value = centered * scale
        if source is feats:
            normed[...] = value
            inv_std[...] = scale
            hidden[...] = (value * gain[...]).astype(BF)
        else:
            hidden_peer[...] = (value * gain[...]).astype(BF)


def picked_kernel(ids, place_ref, hidden, mine, theirs):
    place = place_ref[...]
    index = lax.broadcasted_iota(jnp.int32, (256, 1), 0)
    inside = index & 15
    for k in range(4):
        for core, out in ((ids[1], mine), (1 - ids[1], theirs)):
            shard = (index >> 7) * 16 + ((index >> 4) & 7) * 2 + core
            found = shard * 56 + ((ids[0] + k) & 3) * 14 + inside
            found = jnp.where(inside < 14, found, -1)
            choose = jnp.where(found == place, 1.0, 0.0).astype(BF)
            part = lax.dot_general(choose, hidden[...], LAST, preferred_element_type=F32)
            out[k * 256 : (k + 1) * 256] = part.astype(BF)


def projection_kernel(
    hidden, hidden_peer, weight_mine, weight_other, image_bf, image_unit, image_norm, peer_bf
):
    half = weight_mine.shape[0]
    for source in (hidden_peer, hidden):
        projected = jnp.dot(source[:, :half], weight_mine[...], preferred_element_type=F32)
        projected = projected + jnp.dot(
            source[:, half:], weight_other[...], preferred_element_type=F32
        )
        norm = jnp.sqrt(jnp.sum(projected * projected, -1, keepdims=True) + 1e-06)
        unit = projected / norm
        if source is hidden:
            image_norm[...] = norm
            image_unit[...] = unit
            image_bf[...] = unit.astype(BF)
        else:
            peer_bf[...] = unit.astype(BF)


def image_grad_kernel(
    place_ref, proj_grad, weight_mine, weight_other, normed_ref, inv_std, gain, out, gain_out
):
    grad = proj_grad[...]
    hidden_grad = jnp.concatenate(
        [
            lax.dot_general(grad, weight[...], LAST, preferred_element_type=F32)
            for weight in (weight_mine, weight_other)
        ],
        1,
    )
    normed = normed_ref[...]
    gain_part = jnp.sum(hidden_grad * normed, 0, keepdims=True)
    high = gain_part.astype(BF)
    gain_part = gain_part - high.astype(F32)
    middle = gain_part.astype(BF)
    low = (gain_part - middle.astype(F32)).astype(BF)
    back = hidden_grad * gain[...]
    result = (
        inv_std[...]
        * (
            back
            - jnp.mean(back, -1, keepdims=True)
            - normed * jnp.mean(back * normed, -1, keepdims=True)
        )
    ).astype(BF)
    place = place_ref[...]
    for k in range(out.shape[1] // 256):
        cut = slice(k * 256, (k + 1) * 256)
        order = order_of(place, k)
        out[:, cut] = lax.dot_general(result, order, LAST, preferred_element_type=F32).astype(BF)
        total = jnp.zeros((1, 256), F32)
        for part in (high, middle, low):
            total = total + lax.dot_general(part, order, LAST, preferred_element_type=F32)
        gain_out[:, cut] = total


def weight_kernel(mine, theirs, grad_mine, grad_theirs, *refs):
    arrived, out = refs[:-1], refs[-1]
    total = jnp.dot(mine[...], grad_mine[...], preferred_element_type=F32)
    total = total + jnp.dot(theirs[...], grad_theirs[...], preferred_element_type=F32)
    for part in arrived:
        total = total + part[...].astype(F32)
    out[...] = total.astype(BF)


def slopes_of(scalars, left, right, own):
    dots = lax.dot_general(left, right, LAST, preferred_element_type=F32)
    logits = scalars[0] * dots + scalars[1]
    if own:
        row_ids = lax.broadcasted_iota(jnp.int32, logits.shape, 0)
        col_ids = lax.broadcasted_iota(jnp.int32, logits.shape, 1)
        signs = jnp.where(row_ids == col_ids, 1.0, -1.0).astype(F32)
        slopes = -signs * jax.nn.sigmoid(-signs * logits)
    else:
        slopes = jax.nn.sigmoid(logits)
    return slopes.astype(BF)


def image_part_kernel(own, scalars, image_bf, *refs):
    texts, out = refs[:4], refs[4]
    images = image_bf[...]
    total = jnp.zeros(out.shape, F32)
    for k in range(4):
        block = texts[k][...]
        slopes = slopes_of(scalars, images, block, own and k == 0)
        total = total + jnp.dot(slopes, block, preferred_element_type=F32)
    out[...] = (scalars[0] * total).astype(out.dtype)


def proj_grad_kernel(image_unit, image_norm, own, arrived, out):
    unit = image_unit[...]
    total = own[...] + arrived[...].astype(F32)
    along = jnp.sum(unit * total, -1, keepdims=True)
    out[...] = ((total - unit * along) / image_norm[...]).astype(BF)


def text_kernel(scalars, image_own, image_peer, *refs):
    texts, outs = refs[:4], refs[4:]
    own, peer = image_own[...], image_peer[...]
    for k in (1, 2, 3, 0):
        block = texts[k][...]
        part = jnp.dot(slopes_of(scalars, block, own, k == 0), own, preferred_element_type=F32)
        part = part + jnp.dot(
            slopes_of(scalars, block, peer, False), peer, preferred_element_type=F32
        )
        outs[k][...] = (scalars[0] * part).astype(outs[k].dtype)


def local_call(kernel, outs, inputs, scalars=0):
    spaces = [pltpu.SMEM] * scalars + [pltpu.VMEM] * (len(inputs) - scalars)
    results = pl.pallas_call(
        kernel,
        out_shape=[jax.ShapeDtypeStruct(shape, kind) for shape, kind in outs],
        in_specs=[pl.BlockSpec(memory_space=space) for space in spaces],
        out_specs=[pl.BlockSpec(memory_space=pltpu.VMEM)] * len(outs),
        compiler_params=pltpu.CompilerParams(vmem_limit_bytes=VMEM_BYTES),
        cost_estimate=pl.CostEstimate(flops=1, bytes_accessed=1, transcendentals=0),
    )(*inputs)
    return results[0] if len(outs) == 1 else results


def body(image_feats, text_emb, ln_gain, proj_weight, log_temp, bias):
    rows, feat_width = image_feats.shape
    width = proj_weight.shape[1]
    block = (rows, width)
    y, xl, z, c = (lax.axis_index(name) for name in ("y", "xl", "z", "c"))
    scalars = jnp.stack([jnp.exp(log_temp[0]), bias[0]])
    ids = jnp.stack([y, c])
    place = weight_row(lax.broadcasted_iota(jnp.int32, (1, feat_width), 1), c, xl, z)
    gains = jnp.pad(in_three(ln_gain), ((0, 13), (0, 0)))

    near_z = [moved(proj_weight, "z", by) for by in (1, -1, 2, -2)]
    feats_peer = moved(image_feats, "xh", 1)
    text_bf = local_call(text_unit_kernel, [(block, BF)], [text_emb])

    down_1, up_1, down_2, up_2 = after(near_z, text_bf)
    below = jnp.concatenate([down_1, down_2[:32]])
    above = jnp.concatenate([up_1, up_2[32:]])
    first = jnp.concatenate([proj_weight, down_1, up_1, down_2])
    text_bf, first = after((text_bf, first), below, above)
    below, above = moved(below, "z", 2), moved(above, "z", -2)
    other_first = moved(first, ROW, 1)
    near = around(text_bf, "y")
    second = [up_2, below[:56], above[:56], below[56:], above[56:]]
    second = jnp.concatenate(second)
    second = after(second, below)
    other_second = moved(second, ROW, -1)

    wide = image_feats.shape
    hidden, normed, inv_std, gain, hidden_peer = local_call(
        layer_norm_kernel,
        [(wide, BF), (wide, F32), ((rows, 1), F32), ((1, feat_width), F32), (wide, BF)],
        [place, gains, after(image_feats, second), feats_peer],
    )

    others = after([other_first, other_second], hidden, near)
    weight_mine = jnp.concatenate([first, second] + others)
    weight_other = moved(weight_mine, "c", 1)

    mine, theirs = local_call(
        picked_kernel,
        [((1024, rows), BF)] * 2,
        [ids, place, after(hidden, weight_mine)],
        1,
    )
    theirs = moved(theirs, "c", 1)
    image_bf, image_unit, image_norm, peer_bf = local_call(
        projection_kernel,
        [(block, BF), (block, F32), ((rows, 1), F32), (block, BF)],
        [hidden, hidden_peer, weight_mine, after(weight_other, mine)],
    )

    texts = [text_bf] + near
    peer_part = local_call(
        functools.partial(image_part_kernel, False), [(block, BF)], [scalars, peer_bf] + texts, 1
    )
    arrived_part = moved(peer_part, "xh", 1)
    text_parts = local_call(
        text_kernel,
        [(block, F32 if k == 0 else BF) for k in range(4)],
        [after(scalars, peer_part), image_bf, peer_bf] + texts,
        1,
    )
    own_part = local_call(
        functools.partial(image_part_kernel, True),
        [(block, F32)],
        [after(scalars, text_parts), image_bf] + texts,
        1,
    )
    proj_grad = local_call(
        proj_grad_kernel, [(block, BF)], [image_unit, image_norm, own_part, arrived_part]
    )
    other_grad = moved(proj_grad, "c", 1)

    mine, theirs = mine.reshape(4, rows, rows), theirs.reshape(4, rows, rows)
    sends = [
        local_call(weight_kernel, [(block, BF)], [mine[k], theirs[k], proj_grad, other_grad])
        for k in (1, 2, 3)
    ]
    arrived = [moved(sends[k - 1], "y", k) for k in (1, 2, 3)]

    image_grad, gain_part = local_call(
        image_grad_kernel,
        [(wide, BF), ((1, feat_width), F32)],
        [place, after(proj_grad, sends), weight_mine, weight_other, normed, inv_std, gain],
    )
    gain_part = jnp.pad(gain_part[0], (0, 256)).reshape(16, 128)
    gain_part = jnp.broadcast_to(gain_part, (32, 16, 128))
    gain_part = jnp.sum(lax.all_to_all(gain_part, FSDP, 0, 0, tiled=True), 0)
    arrived = after(arrived, image_grad, gain_part)
    total = local_call(
        weight_kernel, [(block, BF)], [mine[0], theirs[0], proj_grad, other_grad] + arrived
    )
    shared = lax.all_to_all(total.reshape(16, 16, width), ("xl", "z"), 0, 0, tiled=True)
    text_sends = after(text_parts[1:], total)
    text_arrived = [moved(text_sends[k - 1], "y", k) for k in (1, 2, 3)]
    gain_part = after(gain_part, total)
    for axis, bit in (("xh", 1), ("y", 1), ("y", 2)):
        gain_part = gain_part + swapped(gain_part, axis, bit)
    piece = jnp.sum(after(shared, gain_part).astype(F32), 0)
    piece = piece + swapped(piece, "xh", 1)
    pieces = piece
    for bit in (1, 2):
        other = swapped(pieces, "y", bit)
        pieces = jnp.where(
            y & bit == 0, jnp.concatenate([pieces, other]), jnp.concatenate([other, pieces])
        )
    weight_grad = pieces.reshape(4, 16, width)[:, :14].reshape(56, width)
    text_grad = local_call(
        text_grad_kernel, [(block, BF)], [after(text_emb, piece), text_parts[0]] + text_arrived
    )
    gain_grad = gain_part.reshape(2048)[:feat_width]
    return (image_grad, text_grad, weight_grad, gain_grad)


def solution(mesh):
    fine = Mesh(mesh.devices.reshape(4, 2, 2, 8, 2), AXES)
    whole = P(AXES, None)
    in_specs = (whole, whole, P(), P(FSDP, None), P(), P())
    out_specs = (whole, whole, P(FSDP, None), P())
    return jax.shard_map(body, mesh=fine, in_specs=in_specs, out_specs=out_specs, check_vma=False)
```

```python
import functools

import jax
import jax.numpy as jnp
from jax import lax
from jax.experimental import pallas as pl
from jax.experimental.pallas import tpu as pltpu
from jax.sharding import Mesh, PartitionSpec as P

AXES = ("y", "xh", "xl", "z", "c")
FSDP = ("xl", "z", "c")
ROW = ("xh", "xl")
BF = jnp.bfloat16
F32 = jnp.float32
VMEM_BYTES = 20 * 1024 * 1024
LAST = (((1,), (1,)), ((), ()))


def moved(value, axis, by):
    devices = lax.axis_size(axis)
    return lax.ppermute(value, axis, [(i, (i + by) % devices) for i in range(devices)])


def around(value, axis):
    return [moved(value, axis, -k) for k in (1, 2, 3)]


def after(value, *others):
    return lax.optimization_barrier((value, others))[0]


def swapped(value, axis, bit):
    devices = lax.axis_size(axis)
    return lax.ppermute(value, axis, [(i, i ^ bit) for i in range(devices)])


def in_three(vector):
    high = lax.reduce_precision(vector, 8, 7)
    middle = lax.reduce_precision(vector - high, 8, 7)
    return jnp.stack([high, middle, vector - high - middle]).astype(BF)


def weight_row(place, core, xl, z):
    core = (core + place // 896) % 2
    xl = (xl + place // 448 % 2) % 2
    block = place // 56 % 8
    away = (block + 1) // 2
    z = (z + jnp.where(block % 2 == 1, 8 - away, away)) % 8
    return (xl * 16 + z * 2 + core) * 56 + place % 56


def text_unit_of(text):
    wide = text[...].astype(F32)
    norm = jnp.sqrt(jnp.sum(wide * wide, -1, keepdims=True) + 1e-06)
    return wide / norm, norm


def text_unit_kernel(text, out):
    out[...] = text_unit_of(text)[0].astype(BF)


def text_grad_kernel(text, own, *refs):
    arrived, out = refs[:-1], refs[-1]
    unit, norm = text_unit_of(text)
    total = own[...]
    for part in arrived:
        total = total + part[...].astype(F32)
    along = jnp.sum(unit * total, -1, keepdims=True)
    out[...] = ((total - unit * along) / norm).astype(BF)


def order_of(place, k):
    rows = lax.broadcasted_iota(jnp.int32, (256, place.shape[1]), 0) + k * 256
    return jnp.where(rows == place, 1.0, 0.0).astype(BF)


def layer_norm_kernel(
    place_ref, gains, feats, feats_peer, hidden, normed, inv_std, gain, hidden_peer
):
    place = place_ref[...]
    gain_parts = jnp.zeros(gains.shape, F32)
    for source in (feats, feats_peer):
        value = jnp.zeros(feats.shape, F32)
        for k in range(feats.shape[1] // 256):
            cut = slice(k * 256, (k + 1) * 256)
            order = order_of(place, k)
            value = value + jnp.dot(source[:, cut], order, preferred_element_type=F32)
            if source is feats:
                gain_parts = gain_parts + jnp.dot(
                    gains[:, cut], order, preferred_element_type=F32
                )
        if source is feats:
            gain[...] = jnp.sum(gain_parts, 0, keepdims=True)
        centered = value - jnp.mean(value, -1, keepdims=True)
        scale = lax.rsqrt(jnp.mean(centered * centered, -1, keepdims=True) + 1e-06)
        value = centered * scale
        if source is feats:
            normed[...] = value
            inv_std[...] = scale
            hidden[...] = (value * gain[...]).astype(BF)
        else:
            hidden_peer[...] = (value * gain[...]).astype(BF)


def picked_kernel(ids, place_ref, hidden, mine, theirs):
    place = place_ref[...]
    index = lax.broadcasted_iota(jnp.int32, (256, 1), 0)
    inside = index & 7
    for k in range(4):
        for core, out in ((ids[1], mine), (1 - ids[1], theirs)):
            to_x = (ids[0] + k) & 3
            shard = (to_x & 1) * 16 + ((index >> 3) & 7) * 2 + core
            found = shard * 56 + (to_x >> 1) * 28 + (index >> 6) * 7 + inside
            found = jnp.where(inside < 7, found, -1)
            choose = jnp.where(found == place, 1.0, 0.0).astype(BF)
            part = lax.dot_general(choose, hidden[...], LAST, preferred_element_type=F32)
            out[k * 256 : (k + 1) * 256] = part.astype(BF)


def projection_kernel(
    hidden, hidden_peer, weight_mine, weight_other, image_bf, image_unit, image_norm, peer_bf
):
    half = weight_mine.shape[0]
    for source in (hidden_peer, hidden):
        projected = jnp.dot(source[:, :half], weight_mine[...], preferred_element_type=F32)
        projected = projected + jnp.dot(
            source[:, half:], weight_other[...], preferred_element_type=F32
        )
        norm = jnp.sqrt(jnp.sum(projected * projected, -1, keepdims=True) + 1e-06)
        unit = projected / norm
        if source is hidden:
            image_norm[...] = norm
            image_unit[...] = unit
            image_bf[...] = unit.astype(BF)
        else:
            peer_bf[...] = unit.astype(BF)


def hidden_grad_kernel(
    place_ref, proj_grad, weight_mine, weight_other, normed_ref, inv_std, gain, out, gain_out
):
    grad = proj_grad[...]
    hidden_grad = jnp.concatenate(
        [
            lax.dot_general(grad, weight[...], LAST, preferred_element_type=F32)
            for weight in (weight_mine, weight_other)
        ],
        1,
    )
    normed = normed_ref[...]
    gain_part = jnp.sum(hidden_grad * normed, 0, keepdims=True)
    high = gain_part.astype(BF)
    gain_part = gain_part - high.astype(F32)
    middle = gain_part.astype(BF)
    low = (gain_part - middle.astype(F32)).astype(BF)
    parts = jnp.concatenate([high, middle, low, jnp.zeros((13, high.shape[1]), BF)])
    place = place_ref[...]
    for k in range(out.shape[1] // 256):
        cut = slice(k * 256, (k + 1) * 256)
        found = lax.dot_general(parts, order_of(place, k), LAST, preferred_element_type=F32)
        gain_out[:, cut] = jnp.sum(found, 0, keepdims=True)
    back = hidden_grad * gain[...]
    out[...] = (
        inv_std[...]
        * (
            back
            - jnp.mean(back, -1, keepdims=True)
            - normed * jnp.mean(back * normed, -1, keepdims=True)
        )
    ).astype(BF)


def in_order_kernel(place_ref, grad, out):
    place = place_ref[...]
    for k in range(out.shape[1] // 256):
        cut = slice(k * 256, (k + 1) * 256)
        order = order_of(place, k)
        out[:, cut] = lax.dot_general(
            grad[...], order, LAST, preferred_element_type=F32
        ).astype(BF)


def weight_kernel(mine, theirs, grad_mine, grad_theirs, *refs):
    arrived, out = refs[:-1], refs[-1]
    total = jnp.dot(mine[...], grad_mine[...], preferred_element_type=F32)
    total = total + jnp.dot(theirs[...], grad_theirs[...], preferred_element_type=F32)
    for part in arrived:
        total = total + part[...].astype(F32)
    out[...] = total.astype(BF)


def slopes_of(scalars, left, right, own):
    dots = lax.dot_general(left, right, LAST, preferred_element_type=F32)
    logits = scalars[0] * dots + scalars[1]
    if own:
        row_ids = lax.broadcasted_iota(jnp.int32, logits.shape, 0)
        col_ids = lax.broadcasted_iota(jnp.int32, logits.shape, 1)
        signs = jnp.where(row_ids == col_ids, 1.0, -1.0).astype(F32)
        slopes = -signs * jax.nn.sigmoid(-signs * logits)
    else:
        slopes = jax.nn.sigmoid(logits)
    return slopes.astype(BF)


def image_part_kernel(own, scalars, image_bf, *refs):
    texts, out = refs[:4], refs[4]
    images = image_bf[...]
    total = jnp.zeros(out.shape, F32)
    for k in range(4):
        block = texts[k][...]
        slopes = slopes_of(scalars, images, block, own and k == 0)
        total = total + jnp.dot(slopes, block, preferred_element_type=F32)
    out[...] = (scalars[0] * total).astype(out.dtype)


def proj_grad_kernel(image_unit, image_norm, own, arrived, out):
    unit = image_unit[...]
    total = own[...] + arrived[...].astype(F32)
    along = jnp.sum(unit * total, -1, keepdims=True)
    out[...] = ((total - unit * along) / image_norm[...]).astype(BF)


def text_kernel(scalars, image_own, image_peer, *refs):
    texts, outs = refs[:4], refs[4:]
    own, peer = image_own[...], image_peer[...]
    for k in (1, 2, 3, 0):
        block = texts[k][...]
        part = jnp.dot(slopes_of(scalars, block, own, k == 0), own, preferred_element_type=F32)
        part = part + jnp.dot(
            slopes_of(scalars, block, peer, False), peer, preferred_element_type=F32
        )
        outs[k][...] = (scalars[0] * part).astype(outs[k].dtype)


def local_call(kernel, outs, inputs, scalars=0):
    spaces = [pltpu.SMEM] * scalars + [pltpu.VMEM] * (len(inputs) - scalars)
    results = pl.pallas_call(
        kernel,
        out_shape=[jax.ShapeDtypeStruct(shape, kind) for shape, kind in outs],
        in_specs=[pl.BlockSpec(memory_space=space) for space in spaces],
        out_specs=[pl.BlockSpec(memory_space=pltpu.VMEM)] * len(outs),
        compiler_params=pltpu.CompilerParams(vmem_limit_bytes=VMEM_BYTES),
        cost_estimate=pl.CostEstimate(flops=1, bytes_accessed=1, transcendentals=0),
    )(*inputs)
    return results[0] if len(outs) == 1 else results


def body(image_feats, text_emb, ln_gain, proj_weight, log_temp, bias):
    rows, feat_width = image_feats.shape
    width = proj_weight.shape[1]
    block = (rows, width)
    xl, z, c = (lax.axis_index(name) for name in ("xl", "z", "c"))
    scalars = jnp.stack([jnp.exp(log_temp[0]), bias[0]])
    ids = jnp.stack([lax.axis_index(ROW), c])
    place = weight_row(lax.broadcasted_iota(jnp.int32, (1, feat_width), 1), c, xl, z)
    gains = jnp.pad(in_three(ln_gain), ((0, 13), (0, 0)))

    near_z = [moved(proj_weight, "z", by) for by in (1, -1, 2, -2)]
    feats_peer = moved(image_feats, "xh", 1)
    text_bf = local_call(text_unit_kernel, [(block, BF)], [text_emb])

    down_1, up_1, down_2, up_2 = after(near_z, text_bf)
    below = jnp.concatenate([down_1, down_2[:32]])
    above = jnp.concatenate([up_1, up_2[32:]])
    first = jnp.concatenate([proj_weight, down_1, up_1, down_2])
    text_bf, first = after((text_bf, first), below, above)
    below, above = moved(below, "z", 2), moved(above, "z", -2)
    other_first = moved(first, ROW, 1)
    near = around(text_bf, "y")
    second = [up_2, below[:56], above[:56], below[56:], above[56:]]
    second = jnp.concatenate(second)
    second = after(second, below)
    other_second = moved(second, ROW, -1)

    wide = image_feats.shape
    hidden, normed, inv_std, gain, hidden_peer = local_call(
        layer_norm_kernel,
        [(wide, BF), (wide, F32), ((rows, 1), F32), ((1, feat_width), F32), (wide, BF)],
        [place, gains, after(image_feats, second), feats_peer],
    )

    others = after([other_first, other_second], hidden, near)
    weight_mine = jnp.concatenate([first, second] + others)
    weight_other = moved(weight_mine, "c", 1)

    mine, theirs = local_call(
        picked_kernel,
        [((1024, rows), BF)] * 2,
        [ids, place, after(hidden, weight_mine)],
        1,
    )
    theirs = moved(theirs, "c", 1)
    image_bf, image_unit, image_norm, peer_bf = local_call(
        projection_kernel,
        [(block, BF), (block, F32), ((rows, 1), F32), (block, BF)],
        [hidden, hidden_peer, weight_mine, after(weight_other, theirs)],
    )

    texts = [text_bf] + near
    peer_part = local_call(
        functools.partial(image_part_kernel, False), [(block, BF)], [scalars, peer_bf] + texts, 1
    )
    arrived_part = moved(peer_part, "xh", 1)
    text_parts = local_call(
        text_kernel,
        [(block, F32 if k == 0 else BF) for k in range(4)],
        [after(scalars, peer_part), image_bf, peer_bf] + texts,
        1,
    )
    own_part = local_call(
        functools.partial(image_part_kernel, True),
        [(block, F32)],
        [after(scalars, text_parts), image_bf] + texts,
        1,
    )
    proj_grad = local_call(
        proj_grad_kernel, [(block, BF)], [image_unit, image_norm, own_part, arrived_part]
    )
    other_grad = moved(proj_grad, "c", 1)

    mine, theirs = mine.reshape(4, rows, rows), theirs.reshape(4, rows, rows)
    sends = [
        local_call(weight_kernel, [(block, BF)], [mine[k], theirs[k], proj_grad, other_grad])
        for k in (1, 2, 3)
    ]
    arrived = [moved(sends[k - 1], ROW, k) for k in (1, 2, 3)]

    text_sends = after(text_parts[1:3], sends)
    text_arrived = [moved(text_sends[k - 1], "y", k) for k in (1, 2)]
    image_grad, gain_part = local_call(
        hidden_grad_kernel,
        [(wide, BF), ((1, feat_width), F32)],
        [place, after(proj_grad, sends), weight_mine, weight_other, normed, inv_std, gain],
    )
    gain_part = jnp.pad(gain_part[0], (0, 256)).reshape(16, 128)
    gain_part = jnp.broadcast_to(gain_part, (16, 16, 128))
    gain_part = jnp.sum(lax.all_to_all(gain_part, ("z", "c"), 0, 0, tiled=True), 0)

    arrived = after(arrived, text_arrived, gain_part)
    total = local_call(
        weight_kernel, [(block, BF)], [mine[0], theirs[0], proj_grad, other_grad] + arrived
    )
    shared = lax.all_to_all(total.reshape(32, 8, width), ("y", "z"), 0, 0, tiled=True)

    text_arrived.append(moved(after(text_parts[3], total), "y", 3))
    gain_part = after(gain_part, total)
    for axis, bit in (("xl", 1), ("xh", 1), ("y", 1), ("y", 2)):
        gain_part = gain_part + swapped(gain_part, axis, bit)
    image_grad = local_call(in_order_kernel, [(wide, BF)], [place, after(image_grad, total)])

    piece = jnp.sum(after(shared, gain_part, text_arrived[2], image_grad).astype(F32), 0)
    pieces = piece
    for axis, bit in (("y", 1), ("y", 2), ("xh", 1)):
        other = swapped(pieces, axis, bit)
        pieces = jnp.where(
            lax.axis_index(axis) & bit == 0,
            jnp.concatenate([pieces, other]),
            jnp.concatenate([other, pieces]),
        )
    weight_grad = pieces.reshape(8, 8, width)[:, :7].reshape(56, width)
    text_grad = local_call(
        text_grad_kernel, [(block, BF)], [after(text_emb, piece), text_parts[0]] + text_arrived
    )
    gain_grad = gain_part.reshape(2048)[:feat_width]
    return (image_grad, text_grad, weight_grad, gain_grad)


def solution(mesh):
    fine = Mesh(mesh.devices.reshape(4, 2, 2, 8, 2), AXES)
    whole = P(AXES, None)
    in_specs = (whole, whole, P(), P(FSDP, None), P(), P())
    out_specs = (whole, whole, P(FSDP, None), P())
    return jax.shard_map(body, mesh=fine, in_specs=in_specs, out_specs=out_specs, check_vma=False)
```

```python
import functools

import jax
import jax.numpy as jnp
from jax import lax
from jax.experimental import pallas as pl
from jax.experimental.pallas import tpu as pltpu
from jax.sharding import Mesh, PartitionSpec as P

AXES = ("y", "xh", "xl", "z", "c")
FSDP = ("xl", "z", "c")
ROW = ("xh", "xl")
BF = jnp.bfloat16
F32 = jnp.float32
VMEM_BYTES = 20 * 1024 * 1024
LAST = (((1,), (1,)), ((), ()))


def moved(value, axis, by):
    devices = lax.axis_size(axis)
    return lax.ppermute(value, axis, [(i, (i + by) % devices) for i in range(devices)])


def around(value, axis):
    return [moved(value, axis, -k) for k in (1, 2, 3)]


def after(value, *others):
    return lax.optimization_barrier((value, others))[0]


def swapped(value, axis, bit):
    devices = lax.axis_size(axis)
    return lax.ppermute(value, axis, [(i, i ^ bit) for i in range(devices)])


def both_ways(axis, bit, own, other):
    return jnp.where(
        lax.axis_index(axis) & bit == 0,
        jnp.concatenate([own, other]),
        jnp.concatenate([other, own]),
    )


def in_three(vector):
    high = lax.reduce_precision(vector, 8, 7)
    middle = lax.reduce_precision(vector - high, 8, 7)
    return jnp.stack([high, middle, vector - high - middle]).astype(BF)


def weight_row(place, core, xl, z):
    core = (core + place // 896) % 2
    xl = (xl + place // 448 % 2) % 2
    block = place // 56 % 8
    away = (block + 1) // 2
    z = (z + jnp.where(block % 2 == 1, 8 - away, away)) % 8
    return (xl * 16 + z * 2 + core) * 56 + place % 56


def text_unit_of(text):
    wide = text[...].astype(F32)
    norm = jnp.sqrt(jnp.sum(wide * wide, -1, keepdims=True) + 1e-06)
    return wide / norm, norm


def text_unit_kernel(text, out):
    out[...] = text_unit_of(text)[0].astype(BF)


def text_grad_kernel(text, own, *refs):
    arrived, out = refs[:-1], refs[-1]
    unit, norm = text_unit_of(text)
    total = own[...]
    for part in arrived:
        total = total + part[...].astype(F32)
    along = jnp.sum(unit * total, -1, keepdims=True)
    out[...] = ((total - unit * along) / norm).astype(BF)


def order_of(place, k):
    rows = lax.broadcasted_iota(jnp.int32, (256, place.shape[1]), 0) + k * 256
    return jnp.where(rows == place, 1.0, 0.0).astype(BF)


def layer_norm_kernel(
    place_ref, gains, feats, feats_peer, hidden, normed, inv_std, gain, hidden_peer
):
    place = place_ref[...]
    gain_parts = jnp.zeros(gains.shape, F32)
    for source in (feats, feats_peer):
        value = jnp.zeros(feats.shape, F32)
        for k in range(feats.shape[1] // 256):
            cut = slice(k * 256, (k + 1) * 256)
            order = order_of(place, k)
            value = value + jnp.dot(source[:, cut], order, preferred_element_type=F32)
            if source is feats:
                gain_parts = gain_parts + jnp.dot(
                    gains[:, cut], order, preferred_element_type=F32
                )
        if source is feats:
            gain[...] = jnp.sum(gain_parts, 0, keepdims=True)
        centered = value - jnp.mean(value, -1, keepdims=True)
        scale = lax.rsqrt(jnp.mean(centered * centered, -1, keepdims=True) + 1e-06)
        value = centered * scale
        if source is feats:
            normed[...] = value
            inv_std[...] = scale
            hidden[...] = (value * gain[...]).astype(BF)
        else:
            hidden_peer[...] = (value * gain[...]).astype(BF)


def picked_kernel(ids, place_ref, hidden, mine, theirs):
    place = place_ref[...]
    index = lax.broadcasted_iota(jnp.int32, (256, 1), 0)
    inside = index & 7
    for k in range(4):
        for core, out in ((ids[1], mine), (1 - ids[1], theirs)):
            to_x = (ids[0] + k) & 3
            shard = (to_x & 1) * 16 + ((index >> 3) & 7) * 2 + core
            found = shard * 56 + (to_x >> 1) * 28 + (index >> 6) * 7 + inside
            found = jnp.where(inside < 7, found, -1)
            choose = jnp.where(found == place, 1.0, 0.0).astype(BF)
            part = lax.dot_general(choose, hidden[...], LAST, preferred_element_type=F32)
            out[k * 256 : (k + 1) * 256] = part.astype(BF)


def projection_kernel(
    hidden, hidden_peer, weight_mine, weight_other, image_bf, image_unit, image_norm, peer_bf
):
    half = weight_mine.shape[0]
    for source in (hidden_peer, hidden):
        projected = jnp.dot(source[:, :half], weight_mine[...], preferred_element_type=F32)
        projected = projected + jnp.dot(
            source[:, half:], weight_other[...], preferred_element_type=F32
        )
        norm = jnp.sqrt(jnp.sum(projected * projected, -1, keepdims=True) + 1e-06)
        unit = projected / norm
        if source is hidden:
            image_norm[...] = norm
            image_unit[...] = unit
            image_bf[...] = unit.astype(BF)
        else:
            peer_bf[...] = unit.astype(BF)


def hidden_grad_kernel(
    place_ref, proj_grad, weight_mine, weight_other, normed_ref, inv_std, gain, out, gain_out
):
    grad = proj_grad[...]
    hidden_grad = jnp.concatenate(
        [
            lax.dot_general(grad, weight[...], LAST, preferred_element_type=F32)
            for weight in (weight_mine, weight_other)
        ],
        1,
    )
    normed = normed_ref[...]
    gain_part = jnp.sum(hidden_grad * normed, 0, keepdims=True)
    high = gain_part.astype(BF)
    gain_part = gain_part - high.astype(F32)
    middle = gain_part.astype(BF)
    low = (gain_part - middle.astype(F32)).astype(BF)
    parts = jnp.concatenate([high, middle, low, jnp.zeros((13, high.shape[1]), BF)])
    place = place_ref[...]
    for k in range(out.shape[1] // 256):
        cut = slice(k * 256, (k + 1) * 256)
        found = lax.dot_general(parts, order_of(place, k), LAST, preferred_element_type=F32)
        gain_out[:, cut] = jnp.sum(found, 0, keepdims=True)
    back = hidden_grad * gain[...]
    out[...] = (
        inv_std[...]
        * (
            back
            - jnp.mean(back, -1, keepdims=True)
            - normed * jnp.mean(back * normed, -1, keepdims=True)
        )
    ).astype(BF)


def in_order_kernel(place_ref, grad, out):
    place = place_ref[...]
    for k in range(out.shape[1] // 256):
        cut = slice(k * 256, (k + 1) * 256)
        order = order_of(place, k)
        out[:, cut] = lax.dot_general(
            grad[...], order, LAST, preferred_element_type=F32
        ).astype(BF)


def weight_kernel(mine, theirs, grad_mine, grad_theirs, out):
    total = jnp.dot(mine[...], grad_mine[...], preferred_element_type=F32)
    total = total + jnp.dot(theirs[...], grad_theirs[...], preferred_element_type=F32)
    out[...] = total.astype(BF)


def weight_sum_kernel(mine, theirs, grad_mine, grad_theirs, gain_row, *refs):
    arrived, out = refs[:-1], refs[-1]
    total = jnp.dot(mine[...], grad_mine[...], preferred_element_type=F32)
    total = total + jnp.dot(theirs[...], grad_theirs[...], preferred_element_type=F32)
    for part in arrived:
        total = total + part[...].astype(F32)
    index = lax.broadcasted_iota(jnp.int32, total.shape, 0)
    out[...] = jnp.where(index & 7 == 7, gain_row[...], total).astype(BF)


def slopes_of(scalars, left, right, own):
    dots = lax.dot_general(left, right, LAST, preferred_element_type=F32)
    logits = scalars[0] * dots + scalars[1]
    if own:
        row_ids = lax.broadcasted_iota(jnp.int32, logits.shape, 0)
        col_ids = lax.broadcasted_iota(jnp.int32, logits.shape, 1)
        signs = jnp.where(row_ids == col_ids, 1.0, -1.0).astype(F32)
        slopes = -signs * jax.nn.sigmoid(-signs * logits)
    else:
        slopes = jax.nn.sigmoid(logits)
    return slopes.astype(BF)


def image_part_kernel(own, scalars, image_bf, *refs):
    texts, out = refs[:4], refs[4]
    images = image_bf[...]
    total = jnp.zeros(out.shape, F32)
    for k in range(4):
        block = texts[k][...]
        slopes = slopes_of(scalars, images, block, own and k == 0)
        total = total + jnp.dot(slopes, block, preferred_element_type=F32)
    out[...] = (scalars[0] * total).astype(out.dtype)


def proj_grad_kernel(image_unit, image_norm, own, arrived, out):
    unit = image_unit[...]
    total = own[...] + arrived[...].astype(F32)
    along = jnp.sum(unit * total, -1, keepdims=True)
    out[...] = ((total - unit * along) / image_norm[...]).astype(BF)


def text_kernel(scalars, image_own, image_peer, *refs):
    texts, outs = refs[:4], refs[4:]
    own, peer = image_own[...], image_peer[...]
    for k in (1, 2, 3, 0):
        block = texts[k][...]
        part = jnp.dot(slopes_of(scalars, block, own, k == 0), own, preferred_element_type=F32)
        part = part + jnp.dot(
            slopes_of(scalars, block, peer, False), peer, preferred_element_type=F32
        )
        outs[k][...] = (scalars[0] * part).astype(outs[k].dtype)


def local_call(kernel, outs, inputs, scalars=0):
    spaces = [pltpu.SMEM] * scalars + [pltpu.VMEM] * (len(inputs) - scalars)
    results = pl.pallas_call(
        kernel,
        out_shape=[jax.ShapeDtypeStruct(shape, kind) for shape, kind in outs],
        in_specs=[pl.BlockSpec(memory_space=space) for space in spaces],
        out_specs=[pl.BlockSpec(memory_space=pltpu.VMEM)] * len(outs),
        compiler_params=pltpu.CompilerParams(vmem_limit_bytes=VMEM_BYTES),
        cost_estimate=pl.CostEstimate(flops=1, bytes_accessed=1, transcendentals=0),
    )(*inputs)
    return results[0] if len(outs) == 1 else results


def body(image_feats, text_emb, ln_gain, proj_weight, log_temp, bias):
    rows, feat_width = image_feats.shape
    width = proj_weight.shape[1]
    block = (rows, width)
    xl, z, c = (lax.axis_index(name) for name in ("xl", "z", "c"))
    scalars = jnp.stack([jnp.exp(log_temp[0]), bias[0]])
    ids = jnp.stack([lax.axis_index(ROW), c])
    place = weight_row(lax.broadcasted_iota(jnp.int32, (1, feat_width), 1), c, xl, z)
    gains = jnp.pad(in_three(ln_gain), ((0, 13), (0, 0)))

    near_z = [moved(proj_weight, "z", by) for by in (1, -1, 2, -2)]
    feats_peer = moved(image_feats, "xh", 1)
    text_bf = local_call(text_unit_kernel, [(block, BF)], [text_emb])

    down_1, up_1, down_2, up_2 = after(near_z, text_bf)
    below = jnp.concatenate([down_1, down_2[:32]])
    above = jnp.concatenate([up_1, up_2[32:]])
    first = jnp.concatenate([proj_weight, down_1, up_1, down_2])
    text_bf, first = after((text_bf, first), below, above)
    below, above = moved(below, "z", 2), moved(above, "z", -2)
    other_first = moved(first, ROW, 1)
    near = around(text_bf, "y")
    second = [up_2, below[:56], above[:56], below[56:], above[56:]]
    second = jnp.concatenate(second)
    second = after(second, below)
    other_second = moved(second, ROW, -1)

    wide = image_feats.shape
    hidden, normed, inv_std, gain, hidden_peer = local_call(
        layer_norm_kernel,
        [(wide, BF), (wide, F32), ((rows, 1), F32), ((1, feat_width), F32), (wide, BF)],
        [place, gains, after(image_feats, second), feats_peer],
    )

    others = after([other_first, other_second], hidden, near)
    weight_mine = jnp.concatenate([first, second] + others)
    weight_other = moved(weight_mine, "c", 1)

    mine, theirs = local_call(
        picked_kernel,
        [((1024, rows), BF)] * 2,
        [ids, place, after(hidden, weight_mine)],
        1,
    )
    theirs = moved(theirs, "c", 1)
    image_bf, image_unit, image_norm, peer_bf = local_call(
        projection_kernel,
        [(block, BF), (block, F32), ((rows, 1), F32), (block, BF)],
        [hidden, hidden_peer, weight_mine, after(weight_other, theirs)],
    )

    texts = [text_bf] + near
    peer_part = local_call(
        functools.partial(image_part_kernel, False), [(block, BF)], [scalars, peer_bf] + texts, 1
    )
    arrived_part = moved(peer_part, "xh", 1)
    text_parts = local_call(
        text_kernel,
        [(block, F32 if k == 0 else BF) for k in range(4)],
        [after(scalars, peer_part), image_bf, peer_bf] + texts,
        1,
    )
    own_part = local_call(
        functools.partial(image_part_kernel, True),
        [(block, F32)],
        [after(scalars, text_parts), image_bf] + texts,
        1,
    )
    proj_grad = local_call(
        proj_grad_kernel, [(block, BF)], [image_unit, image_norm, own_part, arrived_part]
    )
    other_grad = moved(proj_grad, "c", 1)

    mine, theirs = mine.reshape(4, rows, rows), theirs.reshape(4, rows, rows)
    sends = [
        local_call(weight_kernel, [(block, BF)], [mine[k], theirs[k], proj_grad, other_grad])
        for k in (1, 2, 3)
    ]
    arrived = [moved(sends[k - 1], ROW, k) for k in (1, 2, 3)]

    text_sends = after(text_parts[1:3], sends)
    text_arrived = [moved(text_sends[k - 1], "y", k) for k in (1, 2)]
    image_grad, gain_part = local_call(
        hidden_grad_kernel,
        [(wide, BF), ((1, feat_width), F32)],
        [place, after(proj_grad, sends), weight_mine, weight_other, normed, inv_std, gain],
    )
    halves = gain_part.reshape(2, feat_width // 2)
    gain_part = jnp.where(c == 0, halves[0], halves[1])
    gain_part = gain_part + moved(jnp.where(c == 0, halves[1], halves[0]), "c", 1)
    gain_row = jnp.pad(gain_part, (0, width - feat_width // 2))[None]

    total = local_call(
        weight_sum_kernel,
        [(block, BF)],
        [mine[0], theirs[0], proj_grad, other_grad, gain_row] + arrived,
    )
    shared = lax.all_to_all(total.reshape(32, 8, width), ("y", "z"), 0, 0, tiled=True)

    text_arrived.append(moved(after(text_parts[3], total), "y", 3))
    piece = jnp.sum(after(shared, text_arrived).astype(F32), 0)
    image_grad = local_call(in_order_kernel, [(wide, BF)], [place, after(image_grad, piece)])
    other = swapped(piece, "xh", 1)
    gain_part = (piece[7] + other[7])[: feat_width // 2].reshape(7, 128)
    pieces = both_ways("xh", 1, piece, other)
    gain_part = gain_part + swapped(gain_part, "xl", 1)
    pieces = both_ways("y", 1, pieces, swapped(pieces, "y", 1))
    gain_grad = both_ways("c", 1, gain_part, swapped(gain_part, "c", 1)).reshape(feat_width)
    pieces = both_ways("y", 2, pieces, swapped(pieces, "y", 2))
    pieces = pieces.reshape(4, 2, 8, width).transpose(1, 0, 2, 3)
    weight_grad = pieces[:, :, :7].reshape(56, width)
    text_grad = local_call(
        text_grad_kernel, [(block, BF)], [after(text_emb, piece), text_parts[0]] + text_arrived
    )
    return (image_grad, text_grad, weight_grad, gain_grad)


def solution(mesh):
    fine = Mesh(mesh.devices.reshape(4, 2, 2, 8, 2), AXES)
    whole = P(AXES, None)
    in_specs = (whole, whole, P(), P(FSDP, None), P(), P())
    out_specs = (whole, whole, P(FSDP, None), P())
    return jax.shard_map(body, mesh=fine, in_specs=in_specs, out_specs=out_specs, check_vma=False)
```

```python
import functools

import jax
import jax.numpy as jnp
from jax import lax
from jax.experimental import pallas as pl
from jax.experimental.pallas import tpu as pltpu
from jax.sharding import Mesh, PartitionSpec as P

AXES = ("y", "xh", "xl", "z", "c")
FSDP = ("xl", "z", "c")
ROW = ("xh", "xl")
BF = jnp.bfloat16
F32 = jnp.float32
VMEM_BYTES = 20 * 1024 * 1024
LAST = (((1,), (1,)), ((), ()))


def moved(value, axis, by):
    devices = lax.axis_size(axis)
    return lax.ppermute(value, axis, [(i, (i + by) % devices) for i in range(devices)])


def around(value, axis):
    return [moved(value, axis, -k) for k in (1, 2, 3)]


def after(value, *others):
    return lax.optimization_barrier((value, others))[0]


def swapped(value, axis, bit):
    devices = lax.axis_size(axis)
    return lax.ppermute(value, axis, [(i, i ^ bit) for i in range(devices)])


def both_ways(axis, bit, own, other):
    return jnp.where(
        lax.axis_index(axis) & bit == 0,
        jnp.concatenate([own, other]),
        jnp.concatenate([other, own]),
    )


def in_three(vector):
    high = lax.reduce_precision(vector, 8, 7)
    middle = lax.reduce_precision(vector - high, 8, 7)
    return jnp.stack([high, middle, vector - high - middle]).astype(BF)


def weight_row(place, core, xl, z):
    core = (core + place // 896) % 2
    xl = (xl + place // 448 % 2) % 2
    block = place // 56 % 8
    away = (block + 1) // 2
    z = (z + jnp.where(block % 2 == 1, 8 - away, away)) % 8
    return (xl * 16 + z * 2 + core) * 56 + place % 56


def text_unit_of(text):
    wide = text[...].astype(F32)
    norm = jnp.sqrt(jnp.sum(wide * wide, -1, keepdims=True) + 1e-06)
    return wide / norm, norm


def text_unit_kernel(text, out):
    out[...] = text_unit_of(text)[0].astype(BF)


def text_grad_kernel(text, own, *refs):
    arrived, out = refs[:-1], refs[-1]
    unit, norm = text_unit_of(text)
    total = own[...]
    for part in arrived:
        total = total + part[...].astype(F32)
    along = jnp.sum(unit * total, -1, keepdims=True)
    out[...] = ((total - unit * along) / norm).astype(BF)


def order_of(place, k):
    rows = lax.broadcasted_iota(jnp.int32, (256, place.shape[1]), 0) + k * 256
    return jnp.where(rows == place, 1.0, 0.0).astype(BF)


def layer_norm_kernel(
    place_ref, gains, feats, feats_peer, hidden, normed, inv_std, gain, hidden_peer
):
    place = place_ref[...]
    gain_parts = jnp.zeros(gains.shape, F32)
    for source in (feats, feats_peer):
        value = jnp.zeros(feats.shape, F32)
        for k in range(feats.shape[1] // 256):
            cut = slice(k * 256, (k + 1) * 256)
            order = order_of(place, k)
            value = value + jnp.dot(source[:, cut], order, preferred_element_type=F32)
            if source is feats:
                gain_parts = gain_parts + jnp.dot(
                    gains[:, cut], order, preferred_element_type=F32
                )
        if source is feats:
            gain[...] = jnp.sum(gain_parts, 0, keepdims=True)
        centered = value - jnp.mean(value, -1, keepdims=True)
        scale = lax.rsqrt(jnp.mean(centered * centered, -1, keepdims=True) + 1e-06)
        value = centered * scale
        if source is feats:
            normed[...] = value
            inv_std[...] = scale
            hidden[...] = (value * gain[...]).astype(BF)
        else:
            hidden_peer[...] = (value * gain[...]).astype(BF)


def picked_kernel(ids, place_ref, hidden, mine, theirs):
    place = place_ref[...]
    index = lax.broadcasted_iota(jnp.int32, (256, 1), 0)
    inside = index & 7
    for k in range(4):
        for core, out in ((ids[1], mine), (1 - ids[1], theirs)):
            to_x = (ids[0] + k) & 3
            shard = (to_x & 1) * 16 + ((index >> 3) & 7) * 2 + core
            found = shard * 56 + (to_x >> 1) * 28 + (index >> 6) * 7 + inside
            found = jnp.where(inside < 7, found, -1)
            choose = jnp.where(found == place, 1.0, 0.0).astype(BF)
            part = lax.dot_general(choose, hidden[...], LAST, preferred_element_type=F32)
            out[k * 256 : (k + 1) * 256] = part.astype(BF)


def projection_kernel(
    hidden, hidden_peer, weight_mine, weight_other, image_bf, image_unit, image_norm, peer_bf
):
    half = weight_mine.shape[0]
    for source in (hidden_peer, hidden):
        projected = jnp.dot(source[:, :half], weight_mine[...], preferred_element_type=F32)
        projected = projected + jnp.dot(
            source[:, half:], weight_other[...], preferred_element_type=F32
        )
        norm = jnp.sqrt(jnp.sum(projected * projected, -1, keepdims=True) + 1e-06)
        unit = projected / norm
        if source is hidden:
            image_norm[...] = norm
            image_unit[...] = unit
            image_bf[...] = unit.astype(BF)
        else:
            peer_bf[...] = unit.astype(BF)


def hidden_grad_kernel(
    place_ref, proj_grad, weight_mine, weight_other, normed_ref, inv_std, gain, out, gain_out
):
    grad = proj_grad[...]
    hidden_grad = jnp.concatenate(
        [
            lax.dot_general(grad, weight[...], LAST, preferred_element_type=F32)
            for weight in (weight_mine, weight_other)
        ],
        1,
    )
    normed = normed_ref[...]
    gain_part = jnp.sum(hidden_grad * normed, 0, keepdims=True)
    high = gain_part.astype(BF)
    gain_part = gain_part - high.astype(F32)
    middle = gain_part.astype(BF)
    low = (gain_part - middle.astype(F32)).astype(BF)
    parts = jnp.concatenate([high, middle, low, jnp.zeros((13, high.shape[1]), BF)])
    place = place_ref[...]
    for k in range(out.shape[1] // 256):
        cut = slice(k * 256, (k + 1) * 256)
        found = lax.dot_general(parts, order_of(place, k), LAST, preferred_element_type=F32)
        gain_out[:, cut] = jnp.sum(found, 0, keepdims=True)
    back = hidden_grad * gain[...]
    out[...] = (
        inv_std[...]
        * (
            back
            - jnp.mean(back, -1, keepdims=True)
            - normed * jnp.mean(back * normed, -1, keepdims=True)
        )
    ).astype(BF)


def in_order_kernel(place_ref, grad, out):
    place = place_ref[...]
    for k in range(out.shape[1] // 256):
        cut = slice(k * 256, (k + 1) * 256)
        order = order_of(place, k)
        out[:, cut] = lax.dot_general(
            grad[...], order, LAST, preferred_element_type=F32
        ).astype(BF)


def weight_kernel(mine, theirs, grad_mine, grad_theirs, out):
    total = jnp.dot(mine[...], grad_mine[...], preferred_element_type=F32)
    total = total + jnp.dot(theirs[...], grad_theirs[...], preferred_element_type=F32)
    out[...] = total.astype(BF)


def weight_sum_kernel(mine, theirs, grad_mine, grad_theirs, gain_row, *refs):
    arrived, out = refs[:-1], refs[-1]
    total = jnp.dot(mine[...], grad_mine[...], preferred_element_type=F32)
    total = total + jnp.dot(theirs[...], grad_theirs[...], preferred_element_type=F32)
    for part in arrived:
        total = total + part[...].astype(F32)
    index = lax.broadcasted_iota(jnp.int32, total.shape, 0)
    out[...] = jnp.where(index & 7 == 7, gain_row[...], total).astype(BF)


def piece_kernel(shared, out):
    total = jnp.zeros(out.shape, F32)
    for k in range(32):
        total = total + shared[k * 8 : (k + 1) * 8].astype(F32)
    out[...] = total


def join_kernel(ids, own, other, pieces, gain_part):
    low = jnp.where(ids[0] == 0, own[...], other[...])
    pieces[:8] = low
    pieces[8:] = jnp.where(ids[0] == 0, other[...], own[...])
    width = gain_part.shape[1]
    gain_part[...] = own[7:, :width] + other[7:, :width]


def slopes_of(scalars, left, right, own):
    dots = lax.dot_general(left, right, LAST, preferred_element_type=F32)
    logits = scalars[0] * dots + scalars[1]
    if own:
        row_ids = lax.broadcasted_iota(jnp.int32, logits.shape, 0)
        col_ids = lax.broadcasted_iota(jnp.int32, logits.shape, 1)
        signs = jnp.where(row_ids == col_ids, 1.0, -1.0).astype(F32)
        slopes = -signs * jax.nn.sigmoid(-signs * logits)
    else:
        slopes = jax.nn.sigmoid(logits)
    return slopes.astype(BF)


def image_part_kernel(own, scalars, image_bf, *refs):
    texts, out = refs[:4], refs[4]
    images = image_bf[...]
    total = jnp.zeros(out.shape, F32)
    for k in range(4):
        block = texts[k][...]
        slopes = slopes_of(scalars, images, block, own and k == 0)
        total = total + jnp.dot(slopes, block, preferred_element_type=F32)
    out[...] = (scalars[0] * total).astype(out.dtype)


def proj_grad_kernel(image_unit, image_norm, own, arrived, out):
    unit = image_unit[...]
    total = own[...] + arrived[...].astype(F32)
    along = jnp.sum(unit * total, -1, keepdims=True)
    out[...] = ((total - unit * along) / image_norm[...]).astype(BF)


def text_kernel(scalars, image_own, image_peer, *refs):
    texts, outs = refs[:4], refs[4:]
    own, peer = image_own[...], image_peer[...]
    for k in (1, 2, 3, 0):
        block = texts[k][...]
        part = jnp.dot(slopes_of(scalars, block, own, k == 0), own, preferred_element_type=F32)
        part = part + jnp.dot(
            slopes_of(scalars, block, peer, False), peer, preferred_element_type=F32
        )
        outs[k][...] = (scalars[0] * part).astype(outs[k].dtype)


def local_call(kernel, outs, inputs, scalars=0):
    spaces = [pltpu.SMEM] * scalars + [pltpu.VMEM] * (len(inputs) - scalars)
    results = pl.pallas_call(
        kernel,
        out_shape=[jax.ShapeDtypeStruct(shape, kind) for shape, kind in outs],
        in_specs=[pl.BlockSpec(memory_space=space) for space in spaces],
        out_specs=[pl.BlockSpec(memory_space=pltpu.VMEM)] * len(outs),
        compiler_params=pltpu.CompilerParams(vmem_limit_bytes=VMEM_BYTES),
        cost_estimate=pl.CostEstimate(flops=1, bytes_accessed=1, transcendentals=0),
    )(*inputs)
    return results[0] if len(outs) == 1 else results


def body(image_feats, text_emb, ln_gain, proj_weight, log_temp, bias):
    rows, feat_width = image_feats.shape
    width = proj_weight.shape[1]
    block = (rows, width)
    xl, z, c = (lax.axis_index(name) for name in ("xl", "z", "c"))
    scalars = jnp.stack([jnp.exp(log_temp[0]), bias[0]])
    ids = jnp.stack([lax.axis_index(ROW), c])
    place = weight_row(lax.broadcasted_iota(jnp.int32, (1, feat_width), 1), c, xl, z)
    gains = jnp.pad(in_three(ln_gain), ((0, 13), (0, 0)))

    near_z = [moved(proj_weight, "z", by) for by in (1, -1, 2, -2)]
    feats_peer = moved(image_feats, "xh", 1)
    text_bf = local_call(text_unit_kernel, [(block, BF)], [text_emb])

    down_1, up_1, down_2, up_2 = after(near_z, text_bf)
    below = jnp.concatenate([down_1, down_2[:32]])
    above = jnp.concatenate([up_1, up_2[32:]])
    first = jnp.concatenate([proj_weight, down_1, up_1, down_2])
    text_bf, first = after((text_bf, first), below, above)
    below, above = moved(below, "z", 2), moved(above, "z", -2)
    other_first = moved(first, ROW, 1)
    near = around(text_bf, "y")
    second = [up_2, below[:56], above[:56], below[56:], above[56:]]
    second = jnp.concatenate(second)
    second = after(second, below)
    other_second = moved(second, ROW, -1)

    wide = image_feats.shape
    hidden, normed, inv_std, gain, hidden_peer = local_call(
        layer_norm_kernel,
        [(wide, BF), (wide, F32), ((rows, 1), F32), ((1, feat_width), F32), (wide, BF)],
        [place, gains, after(image_feats, second), feats_peer],
    )

    others = after([other_first, other_second], hidden, near)
    weight_mine = jnp.concatenate([first, second] + others)
    weight_other = moved(weight_mine, "c", 1)

    mine, theirs = local_call(
        picked_kernel,
        [((1024, rows), BF)] * 2,
        [ids, place, after(hidden, weight_mine)],
        1,
    )
    theirs = moved(theirs, "c", 1)
    image_bf, image_unit, image_norm, peer_bf = local_call(
        projection_kernel,
        [(block, BF), (block, F32), ((rows, 1), F32), (block, BF)],
        [hidden, hidden_peer, weight_mine, after(weight_other, theirs)],
    )

    texts = [text_bf] + near
    peer_part = local_call(
        functools.partial(image_part_kernel, False), [(block, BF)], [scalars, peer_bf] + texts, 1
    )
    arrived_part = moved(peer_part, "xh", 1)
    text_parts = local_call(
        text_kernel,
        [(block, F32 if k == 0 else BF) for k in range(4)],
        [after(scalars, peer_part), image_bf, peer_bf] + texts,
        1,
    )
    own_part = local_call(
        functools.partial(image_part_kernel, True),
        [(block, F32)],
        [after(scalars, text_parts), image_bf] + texts,
        1,
    )
    proj_grad = local_call(
        proj_grad_kernel, [(block, BF)], [image_unit, image_norm, own_part, arrived_part]
    )
    other_grad = moved(proj_grad, "c", 1)

    mine, theirs = mine.reshape(4, rows, rows), theirs.reshape(4, rows, rows)
    sends = [
        local_call(weight_kernel, [(block, BF)], [mine[k], theirs[k], proj_grad, other_grad])
        for k in (1, 2, 3)
    ]
    arrived = [moved(sends[k - 1], ROW, k) for k in (1, 2, 3)]

    text_arrived = [moved(after(text_parts[2], sends), "y", 2)]
    image_grad, gain_part = local_call(
        hidden_grad_kernel,
        [(wide, BF), ((1, feat_width), F32)],
        [place, after(proj_grad, sends), weight_mine, weight_other, normed, inv_std, gain],
    )
    halves = gain_part.reshape(2, feat_width // 2)
    gain_part = jnp.where(c == 0, halves[0], halves[1])
    gain_part = gain_part + moved(jnp.where(c == 0, halves[1], halves[0]), "c", 1)
    gain_row = jnp.pad(gain_part, (0, width - feat_width // 2))[None]

    arrived = after(arrived, text_arrived)
    total = local_call(
        weight_sum_kernel,
        [(block, BF)],
        [mine[0], theirs[0], proj_grad, other_grad, gain_row] + arrived,
    )
    shared = lax.all_to_all(total.reshape(32, 8, width), ("y", "z"), 0, 0, tiled=True)

    text_arrived.append(moved(after(text_parts[1], total), "y", 1))
    image_grad = local_call(in_order_kernel, [(wide, BF)], [place, after(image_grad, total)])
    text_arrived.append(moved(after(text_parts[3], image_grad), "y", 3))

    piece = local_call(
        piece_kernel, [((8, width), F32)], [after(shared, text_arrived).reshape(256, width)]
    )
    pieces, gain_part = local_call(
        join_kernel,
        [((16, width), F32), ((1, feat_width // 2), F32)],
        [lax.axis_index(("xh",)).reshape(1), piece, swapped(piece, "xh", 1)],
        1,
    )
    gain_part = gain_part + swapped(gain_part, "xl", 1)
    pieces = both_ways("y", 1, pieces, swapped(pieces, "y", 1))
    gain_grad = both_ways("c", 1, gain_part, swapped(gain_part, "c", 1)).reshape(feat_width)
    pieces = both_ways("y", 2, pieces, swapped(pieces, "y", 2))
    pieces = pieces.reshape(4, 2, 8, width).transpose(1, 0, 2, 3)
    weight_grad = pieces[:, :, :7].reshape(56, width)
    text_grad = local_call(
        text_grad_kernel, [(block, BF)], [after(text_emb, piece), text_parts[0]] + text_arrived
    )
    return (image_grad, text_grad, weight_grad, gain_grad)


def solution(mesh):
    fine = Mesh(mesh.devices.reshape(4, 2, 2, 8, 2), AXES)
    whole = P(AXES, None)
    in_specs = (whole, whole, P(), P(FSDP, None), P(), P())
    out_specs = (whole, whole, P(FSDP, None), P())
    return jax.shard_map(body, mesh=fine, in_specs=in_specs, out_specs=out_specs, check_vma=False)
```

```python
import functools

import jax
import jax.numpy as jnp
from jax import lax
from jax.experimental import pallas as pl
from jax.experimental.pallas import tpu as pltpu
from jax.sharding import Mesh, PartitionSpec as P

AXES = ("y", "xh", "xl", "z", "c")
FSDP = ("xl", "z", "c")
ROW = ("xh", "xl")
BF = jnp.bfloat16
F32 = jnp.float32
VMEM_BYTES = 20 * 1024 * 1024
LAST = (((1,), (1,)), ((), ()))


def moved(value, axis, by):
    devices = lax.axis_size(axis)
    return lax.ppermute(value, axis, [(i, (i + by) % devices) for i in range(devices)])


def around(value, axis):
    return [moved(value, axis, -k) for k in (2, 1, 3)]


def after(value, *others):
    return lax.optimization_barrier((value, others))[0]


def swapped(value, axis, bit):
    devices = lax.axis_size(axis)
    return lax.ppermute(value, axis, [(i, i ^ bit) for i in range(devices)])


def both_ways(axis, bit, own, other):
    return jnp.where(
        lax.axis_index(axis) & bit == 0,
        jnp.concatenate([own, other]),
        jnp.concatenate([other, own]),
    )


def in_three(vector):
    high = lax.reduce_precision(vector, 8, 7)
    middle = lax.reduce_precision(vector - high, 8, 7)
    return jnp.stack([high, middle, vector - high - middle]).astype(BF)


def weight_row(place, core, xl, z):
    core = (core + place // 896) % 2
    xl = (xl + place // 448 % 2) % 2
    block = place // 56 % 8
    away = (block + 1) // 2
    z = (z + jnp.where(block % 2 == 1, 8 - away, away)) % 8
    return (xl * 16 + z * 2 + core) * 56 + place % 56


def text_unit_of(text):
    wide = text[...].astype(F32)
    norm = jnp.sqrt(jnp.sum(wide * wide, -1, keepdims=True) + 1e-06)
    return wide / norm, norm


def text_unit_kernel(text, out):
    out[...] = text_unit_of(text)[0].astype(BF)


def text_grad_kernel(text, own, *refs):
    arrived, out = refs[:-1], refs[-1]
    unit, norm = text_unit_of(text)
    total = own[...]
    for part in arrived:
        total = total + part[...].astype(F32)
    along = jnp.sum(unit * total, -1, keepdims=True)
    out[...] = ((total - unit * along) / norm).astype(BF)


def order_of(place, k):
    rows = lax.broadcasted_iota(jnp.int32, (256, place.shape[1]), 0) + k * 256
    return jnp.where(rows == place, 1.0, 0.0).astype(BF)


def layer_norm_kernel(
    place_ref, gains, feats, feats_peer, hidden, normed, inv_std, gain, hidden_peer
):
    place = place_ref[...]
    gain_parts = jnp.zeros(gains.shape, F32)
    for source in (feats, feats_peer):
        value = jnp.zeros(feats.shape, F32)
        for k in range(feats.shape[1] // 256):
            cut = slice(k * 256, (k + 1) * 256)
            order = order_of(place, k)
            value = value + jnp.dot(source[:, cut], order, preferred_element_type=F32)
            if source is feats:
                gain_parts = gain_parts + jnp.dot(
                    gains[:, cut], order, preferred_element_type=F32
                )
        if source is feats:
            gain[...] = jnp.sum(gain_parts, 0, keepdims=True)
        centered = value - jnp.mean(value, -1, keepdims=True)
        scale = lax.rsqrt(jnp.mean(centered * centered, -1, keepdims=True) + 1e-06)
        value = centered * scale
        if source is feats:
            normed[...] = value
            inv_std[...] = scale
            hidden[...] = (value * gain[...]).astype(BF)
        else:
            hidden_peer[...] = (value * gain[...]).astype(BF)


def picked_kernel(ids, place_ref, hidden, mine, theirs):
    place = place_ref[...]
    index = lax.broadcasted_iota(jnp.int32, (256, 1), 0)
    inside = index & 7
    for k in range(4):
        for core, out in ((ids[1], mine), (1 - ids[1], theirs)):
            to_x = (ids[0] + k) & 3
            shard = (to_x & 1) * 16 + ((index >> 3) & 7) * 2 + core
            found = shard * 56 + (to_x >> 1) * 28 + (index >> 6) * 7 + inside
            found = jnp.where(inside < 7, found, -1)
            choose = jnp.where(found == place, 1.0, 0.0).astype(BF)
            part = lax.dot_general(choose, hidden[...], LAST, preferred_element_type=F32)
            out[k * 256 : (k + 1) * 256] = part.astype(BF)


def projection_kernel(
    hidden, hidden_peer, weight_mine, weight_other, image_bf, image_unit, image_norm, peer_bf
):
    half = weight_mine.shape[0]
    for source in (hidden_peer, hidden):
        projected = jnp.dot(source[:, :half], weight_mine[...], preferred_element_type=F32)
        projected = projected + jnp.dot(
            source[:, half:], weight_other[...], preferred_element_type=F32
        )
        norm = jnp.sqrt(jnp.sum(projected * projected, -1, keepdims=True) + 1e-06)
        unit = projected / norm
        if source is hidden:
            image_norm[...] = norm
            image_unit[...] = unit
            image_bf[...] = unit.astype(BF)
        else:
            peer_bf[...] = unit.astype(BF)


def hidden_grad_kernel(
    place_ref, proj_grad, weight_mine, weight_other, normed_ref, inv_std, gain, out, gain_out
):
    grad = proj_grad[...]
    hidden_grad = jnp.concatenate(
        [
            lax.dot_general(grad, weight[...], LAST, preferred_element_type=F32)
            for weight in (weight_mine, weight_other)
        ],
        1,
    )
    normed = normed_ref[...]
    gain_part = jnp.sum(hidden_grad * normed, 0, keepdims=True)
    high = gain_part.astype(BF)
    gain_part = gain_part - high.astype(F32)
    middle = gain_part.astype(BF)
    low = (gain_part - middle.astype(F32)).astype(BF)
    parts = jnp.concatenate([high, middle, low, jnp.zeros((13, high.shape[1]), BF)])
    place = place_ref[...]
    for k in range(out.shape[1] // 256):
        cut = slice(k * 256, (k + 1) * 256)
        found = lax.dot_general(parts, order_of(place, k), LAST, preferred_element_type=F32)
        gain_out[:, cut] = jnp.sum(found, 0, keepdims=True)
    back = hidden_grad * gain[...]
    out[...] = (
        inv_std[...]
        * (
            back
            - jnp.mean(back, -1, keepdims=True)
            - normed * jnp.mean(back * normed, -1, keepdims=True)
        )
    ).astype(BF)


def in_order_kernel(place_ref, grad, out):
    place = place_ref[...]
    for k in range(out.shape[1] // 256):
        cut = slice(k * 256, (k + 1) * 256)
        order = order_of(place, k)
        out[:, cut] = lax.dot_general(
            grad[...], order, LAST, preferred_element_type=F32
        ).astype(BF)


def weight_kernel(mine, theirs, grad_mine, grad_theirs, out):
    total = jnp.dot(mine[...], grad_mine[...], preferred_element_type=F32)
    total = total + jnp.dot(theirs[...], grad_theirs[...], preferred_element_type=F32)
    out[...] = total.astype(BF)


def weight_sum_kernel(mine, theirs, grad_mine, grad_theirs, gain_row, *refs):
    arrived, out = refs[:-1], refs[-1]
    total = jnp.dot(mine[...], grad_mine[...], preferred_element_type=F32)
    total = total + jnp.dot(theirs[...], grad_theirs[...], preferred_element_type=F32)
    for part in arrived:
        total = total + part[...].astype(F32)
    index = lax.broadcasted_iota(jnp.int32, total.shape, 0)
    out[...] = jnp.where(index & 7 == 7, gain_row[...], total).astype(BF)


def piece_kernel(shared, out):
    total = jnp.zeros(out.shape, F32)
    for k in range(32):
        total = total + shared[k * 8 : (k + 1) * 8].astype(F32)
    out[...] = total


def join_kernel(ids, own, other, pieces, gain_part):
    low = jnp.where(ids[0] == 0, own[...], other[...])
    pieces[:8] = low
    pieces[8:] = jnp.where(ids[0] == 0, other[...], own[...])
    width = gain_part.shape[1]
    gain_part[...] = own[7:, :width] + other[7:, :width]


def slopes_of(scalars, left, right, own):
    dots = lax.dot_general(left, right, LAST, preferred_element_type=F32)
    logits = scalars[0] * dots + scalars[1]
    if own:
        row_ids = lax.broadcasted_iota(jnp.int32, logits.shape, 0)
        col_ids = lax.broadcasted_iota(jnp.int32, logits.shape, 1)
        signs = jnp.where(row_ids == col_ids, 1.0, -1.0).astype(F32)
        slopes = -signs * jax.nn.sigmoid(-signs * logits)
    else:
        slopes = jax.nn.sigmoid(logits)
    return slopes.astype(BF)


def image_part_kernel(own, scalars, image_bf, *refs):
    texts, out = refs[:4], refs[4]
    images = image_bf[...]
    total = jnp.zeros(out.shape, F32)
    for k in range(4):
        block = texts[k][...]
        slopes = slopes_of(scalars, images, block, own and k == 0)
        total = total + jnp.dot(slopes, block, preferred_element_type=F32)
    out[...] = (scalars[0] * total).astype(out.dtype)


def proj_grad_kernel(image_unit, image_norm, own, arrived, out):
    unit = image_unit[...]
    total = own[...] + arrived[...].astype(F32)
    along = jnp.sum(unit * total, -1, keepdims=True)
    out[...] = ((total - unit * along) / image_norm[...]).astype(BF)


def text_kernel(scalars, image_own, image_peer, *refs):
    texts, outs = refs[:4], refs[4:]
    own, peer = image_own[...], image_peer[...]
    for k in (1, 2, 3, 0):
        block = texts[k][...]
        part = jnp.dot(slopes_of(scalars, block, own, k == 0), own, preferred_element_type=F32)
        part = part + jnp.dot(
            slopes_of(scalars, block, peer, False), peer, preferred_element_type=F32
        )
        outs[k][...] = (scalars[0] * part).astype(outs[k].dtype)


def local_call(kernel, outs, inputs, scalars=0):
    spaces = [pltpu.SMEM] * scalars + [pltpu.VMEM] * (len(inputs) - scalars)
    results = pl.pallas_call(
        kernel,
        out_shape=[jax.ShapeDtypeStruct(shape, kind) for shape, kind in outs],
        in_specs=[pl.BlockSpec(memory_space=space) for space in spaces],
        out_specs=[pl.BlockSpec(memory_space=pltpu.VMEM)] * len(outs),
        compiler_params=pltpu.CompilerParams(vmem_limit_bytes=VMEM_BYTES),
        cost_estimate=pl.CostEstimate(flops=1, bytes_accessed=1, transcendentals=0),
    )(*inputs)
    return results[0] if len(outs) == 1 else results


def body(image_feats, text_emb, ln_gain, proj_weight, log_temp, bias):
    rows, feat_width = image_feats.shape
    width = proj_weight.shape[1]
    block = (rows, width)
    xl, z, c = (lax.axis_index(name) for name in ("xl", "z", "c"))
    scalars = jnp.stack([jnp.exp(log_temp[0]), bias[0]])
    ids = jnp.stack([lax.axis_index(ROW), c])
    place = weight_row(lax.broadcasted_iota(jnp.int32, (1, feat_width), 1), c, xl, z)
    gains = jnp.pad(in_three(ln_gain), ((0, 13), (0, 0)))

    near_z = [moved(proj_weight, "z", by) for by in (1, -1, 2, -2)]
    feats_peer = moved(image_feats, "xh", 1)
    text_bf = local_call(text_unit_kernel, [(block, BF)], [text_emb])

    down_1, up_1, down_2, up_2 = after(near_z, text_bf)
    below = jnp.concatenate([down_1, down_2[:32]])
    above = jnp.concatenate([up_1, up_2[32:]])
    first = jnp.concatenate([proj_weight, down_1, up_1, down_2])
    text_bf, first = after((text_bf, first), below, above)
    below, above = moved(below, "z", 2), moved(above, "z", -2)
    other_first = moved(first, ROW, 1)
    near = around(text_bf, "y")
    second = [up_2, below[:56], above[:56], below[56:], above[56:]]
    second = jnp.concatenate(second)
    second = after(second, below)
    other_second = moved(second, ROW, -1)

    wide = image_feats.shape
    hidden, normed, inv_std, gain, hidden_peer = local_call(
        layer_norm_kernel,
        [(wide, BF), (wide, F32), ((rows, 1), F32), ((1, feat_width), F32), (wide, BF)],
        [place, gains, after(image_feats, second), feats_peer],
    )

    others = after([other_first, other_second], hidden, near)
    weight_mine = jnp.concatenate([first, second] + others)
    weight_other = moved(weight_mine, "c", 1)

    mine, theirs = local_call(
        picked_kernel,
        [((1024, rows), BF)] * 2,
        [ids, place, after(hidden, weight_mine)],
        1,
    )
    theirs = moved(theirs, "c", 1)
    image_bf, image_unit, image_norm, peer_bf = local_call(
        projection_kernel,
        [(block, BF), (block, F32), ((rows, 1), F32), (block, BF)],
        [hidden, hidden_peer, weight_mine, after(weight_other, theirs)],
    )

    texts = [text_bf] + near
    peer_part = local_call(
        functools.partial(image_part_kernel, False), [(block, BF)], [scalars, peer_bf] + texts, 1
    )
    arrived_part = moved(peer_part, "xh", 1)
    text_parts = local_call(
        text_kernel,
        [(block, F32 if k == 0 else BF) for k in range(4)],
        [after(scalars, peer_part), image_bf, peer_bf] + texts,
        1,
    )
    own_part = local_call(
        functools.partial(image_part_kernel, True),
        [(block, F32)],
        [after(scalars, text_parts), image_bf] + texts,
        1,
    )
    proj_grad = local_call(
        proj_grad_kernel, [(block, BF)], [image_unit, image_norm, own_part, arrived_part]
    )
    other_grad = moved(proj_grad, "c", 1)

    mine, theirs = mine.reshape(4, rows, rows), theirs.reshape(4, rows, rows)
    sends = [
        local_call(weight_kernel, [(block, BF)], [mine[k], theirs[k], proj_grad, other_grad])
        for k in (2, 1, 3)
    ]
    arrived = [moved(send, ROW, k) for k, send in zip((2, 1, 3), sends)]

    text_arrived = [moved(after(text_parts[1], sends), "y", 2)]
    image_grad, gain_part = local_call(
        hidden_grad_kernel,
        [(wide, BF), ((1, feat_width), F32)],
        [place, after(proj_grad, sends), weight_mine, weight_other, normed, inv_std, gain],
    )
    image_grad = local_call(in_order_kernel, [(wide, BF)], [place, image_grad])
    halves = gain_part.reshape(2, feat_width // 2)
    gain_part = jnp.where(c == 0, halves[0], halves[1])
    gain_part = gain_part + moved(jnp.where(c == 0, halves[1], halves[0]), "c", 1)
    gain_row = jnp.pad(gain_part, (0, width - feat_width // 2))[None]

    arrived = after(arrived, text_arrived, image_grad)
    total = local_call(
        weight_sum_kernel,
        [(block, BF)],
        [mine[0], theirs[0], proj_grad, other_grad, gain_row] + arrived,
    )
    shared = lax.all_to_all(total.reshape(32, 8, width), ("y", "z"), 0, 0, tiled=True)

    text_ends = after(text_parts[2:], total)
    text_arrived += [moved(text_ends[0], "y", 1), moved(text_ends[1], "y", 3)]

    piece = local_call(
        piece_kernel, [((8, width), F32)], [after(shared, text_arrived).reshape(256, width)]
    )
    pieces, gain_part = local_call(
        join_kernel,
        [((16, width), F32), ((1, feat_width // 2), F32)],
        [lax.axis_index(("xh",)).reshape(1), piece, swapped(piece, "xh", 1)],
        1,
    )
    gain_part = gain_part + swapped(gain_part, "xl", 1)
    pieces = both_ways("y", 1, pieces, swapped(pieces, "y", 1))
    gain_grad = both_ways("c", 1, gain_part, swapped(gain_part, "c", 1)).reshape(feat_width)
    pieces = after(pieces, gain_part)
    pieces = both_ways("y", 2, pieces, swapped(pieces, "y", 2))
    pieces = pieces.reshape(4, 2, 8, width).transpose(1, 0, 2, 3)
    weight_grad = pieces[:, :, :7].reshape(56, width)
    text_grad = local_call(
        text_grad_kernel, [(block, BF)], [after(text_emb, piece), text_parts[0]] + text_arrived
    )
    return (image_grad, text_grad, weight_grad, gain_grad)


def solution(mesh):
    fine = Mesh(mesh.devices.reshape(4, 2, 2, 8, 2), AXES)
    whole = P(AXES, None)
    in_specs = (whole, whole, P(), P(FSDP, None), P(), P())
    out_specs = (whole, whole, P(FSDP, None), P())
    return jax.shard_map(body, mesh=fine, in_specs=in_specs, out_specs=out_specs, check_vma=False)
```

```python
import functools

import jax
import jax.numpy as jnp
from jax import lax
from jax.experimental import pallas as pl
from jax.experimental.pallas import tpu as pltpu
from jax.sharding import Mesh, PartitionSpec as P

AXES = ("y", "xh", "xl", "z", "c")
FSDP = ("xl", "z", "c")
ROW = ("xh", "xl")
BF = jnp.bfloat16
F32 = jnp.float32
VMEM_BYTES = 20 * 1024 * 1024
LAST = (((1,), (1,)), ((), ()))


def moved(value, axis, by):
    devices = lax.axis_size(axis)
    return lax.ppermute(value, axis, [(i, (i + by) % devices) for i in range(devices)])


def around(value, axis):
    return [moved(value, axis, -k) for k in (2, 1, 3)]


def after(value, *others):
    return lax.optimization_barrier((value, others))[0]


def swapped(value, axis, bit):
    devices = lax.axis_size(axis)
    return lax.ppermute(value, axis, [(i, i ^ bit) for i in range(devices)])


def both_ways(first, own, other):
    return jnp.where(
        first,
        jnp.concatenate([own, other]),
        jnp.concatenate([other, own]),
    )


def in_three(vector):
    high = lax.reduce_precision(vector, 8, 7)
    middle = lax.reduce_precision(vector - high, 8, 7)
    return jnp.stack([high, middle, vector - high - middle]).astype(BF)


def weight_row(place, core, xl, z):
    core = (core + place // 896) % 2
    xl = (xl + place // 448 % 2) % 2
    block = place // 56 % 8
    away = (block + 1) // 2
    z = (z + jnp.where(block % 2 == 1, 8 - away, away)) % 8
    return (xl * 16 + z * 2 + core) * 56 + place % 56


def text_unit_of(text):
    wide = text[...].astype(F32)
    norm = jnp.sqrt(jnp.sum(wide * wide, -1, keepdims=True) + 1e-06)
    return wide / norm, norm


def text_unit_kernel(text, out):
    out[...] = text_unit_of(text)[0].astype(BF)


def text_grad_kernel(text, own, *refs):
    arrived, out = refs[:-1], refs[-1]
    unit, norm = text_unit_of(text)
    total = own[...]
    for part in arrived:
        total = total + part[...].astype(F32)
    along = jnp.sum(unit * total, -1, keepdims=True)
    out[...] = ((total - unit * along) / norm).astype(BF)


def order_of(place, k):
    rows = lax.broadcasted_iota(jnp.int32, (256, place.shape[1]), 0) + k * 256
    return jnp.where(rows == place, 1.0, 0.0).astype(BF)


def layer_norm_kernel(
    place_ref, gains, feats, feats_peer, hidden, normed, inv_std, gain, hidden_peer
):
    place = place_ref[...]
    gain_parts = jnp.zeros(gains.shape, F32)
    for source in (feats, feats_peer):
        value = jnp.zeros(feats.shape, F32)
        for k in range(feats.shape[1] // 256):
            cut = slice(k * 256, (k + 1) * 256)
            order = order_of(place, k)
            value = value + jnp.dot(source[:, cut], order, preferred_element_type=F32)
            if source is feats:
                gain_parts = gain_parts + jnp.dot(
                    gains[:, cut], order, preferred_element_type=F32
                )
        if source is feats:
            gain[...] = jnp.sum(gain_parts, 0, keepdims=True)
        centered = value - jnp.mean(value, -1, keepdims=True)
        scale = lax.rsqrt(jnp.mean(centered * centered, -1, keepdims=True) + 1e-06)
        value = centered * scale
        if source is feats:
            normed[...] = value
            inv_std[...] = scale
            hidden[...] = (value * gain[...]).astype(BF)
        else:
            hidden_peer[...] = (value * gain[...]).astype(BF)


def picked_kernel(ids, place_ref, hidden, mine, theirs):
    place = place_ref[...]
    index = lax.broadcasted_iota(jnp.int32, (256, 1), 0)
    inside = index & 7
    for k in range(4):
        for core, out in ((ids[1], mine), (1 - ids[1], theirs)):
            to_x = (ids[0] + k) & 3
            shard = (to_x & 1) * 16 + ((index >> 3) & 7) * 2 + core
            found = shard * 56 + (to_x >> 1) * 28 + (index >> 6) * 7 + inside
            found = jnp.where(inside < 7, found, -1)
            choose = jnp.where(found == place, 1.0, 0.0).astype(BF)
            part = lax.dot_general(choose, hidden[...], LAST, preferred_element_type=F32)
            out[k * 256 : (k + 1) * 256] = part.astype(BF)


def projection_kernel(
    hidden, hidden_peer, weight_mine, weight_other, image_bf, image_unit, image_norm, peer_bf
):
    half = weight_mine.shape[0]
    for source in (hidden_peer, hidden):
        projected = jnp.dot(source[:, :half], weight_mine[...], preferred_element_type=F32)
        projected = projected + jnp.dot(
            source[:, half:], weight_other[...], preferred_element_type=F32
        )
        norm = jnp.sqrt(jnp.sum(projected * projected, -1, keepdims=True) + 1e-06)
        unit = projected / norm
        if source is hidden:
            image_norm[...] = norm
            image_unit[...] = unit
            image_bf[...] = unit.astype(BF)
        else:
            peer_bf[...] = unit.astype(BF)


def hidden_grad_kernel(
    place_ref, proj_grad, weight_mine, weight_other, normed_ref, inv_std, gain, out, gain_out
):
    grad = proj_grad[...]
    hidden_grad = jnp.concatenate(
        [
            lax.dot_general(grad, weight[...], LAST, preferred_element_type=F32)
            for weight in (weight_mine, weight_other)
        ],
        1,
    )
    normed = normed_ref[...]
    gain_part = jnp.sum(hidden_grad * normed, 0, keepdims=True)
    high = gain_part.astype(BF)
    gain_part = gain_part - high.astype(F32)
    middle = gain_part.astype(BF)
    low = (gain_part - middle.astype(F32)).astype(BF)
    parts = jnp.concatenate([high, middle, low, jnp.zeros((13, high.shape[1]), BF)])
    place = place_ref[...]
    for k in range(out.shape[1] // 256):
        cut = slice(k * 256, (k + 1) * 256)
        found = lax.dot_general(parts, order_of(place, k), LAST, preferred_element_type=F32)
        gain_out[:, cut] = jnp.sum(found, 0, keepdims=True)
    back = hidden_grad * gain[...]
    out[...] = (
        inv_std[...]
        * (
            back
            - jnp.mean(back, -1, keepdims=True)
            - normed * jnp.mean(back * normed, -1, keepdims=True)
        )
    ).astype(BF)


def in_order_kernel(place_ref, grad, out):
    place = place_ref[...]
    for k in range(out.shape[1] // 256):
        cut = slice(k * 256, (k + 1) * 256)
        order = order_of(place, k)
        out[:, cut] = lax.dot_general(
            grad[...], order, LAST, preferred_element_type=F32
        ).astype(BF)


def weight_kernel(mine, theirs, grad_mine, grad_theirs, out):
    total = jnp.dot(mine[...], grad_mine[...], preferred_element_type=F32)
    total = total + jnp.dot(theirs[...], grad_theirs[...], preferred_element_type=F32)
    out[...] = total.astype(BF)


def weight_sum_kernel(mine, theirs, grad_mine, grad_theirs, gain_row, *refs):
    arrived, out = refs[:-1], refs[-1]
    total = jnp.dot(mine[...], grad_mine[...], preferred_element_type=F32)
    total = total + jnp.dot(theirs[...], grad_theirs[...], preferred_element_type=F32)
    for part in arrived:
        total = total + part[...].astype(F32)
    index = lax.broadcasted_iota(jnp.int32, total.shape, 0)
    out[...] = jnp.where(index & 7 == 7, gain_row[...], total).astype(BF)


def piece_kernel(shared, out):
    total = jnp.zeros(out.shape, F32)
    for k in range(32):
        total = total + shared[k * 8 : (k + 1) * 8].astype(F32)
    out[...] = total


def join_kernel(ids, own, other, pieces, gain_part):
    low = jnp.where(ids[0] == 0, own[...], other[...])
    pieces[:8] = low
    pieces[8:] = jnp.where(ids[0] == 0, other[...], own[...])
    width = gain_part.shape[1]
    gain_part[...] = own[7:, :width] + other[7:, :width]


def slopes_of(scalars, left, right, own):
    dots = lax.dot_general(left, right, LAST, preferred_element_type=F32)
    logits = scalars[0] * dots + scalars[1]
    if own:
        row_ids = lax.broadcasted_iota(jnp.int32, logits.shape, 0)
        col_ids = lax.broadcasted_iota(jnp.int32, logits.shape, 1)
        signs = jnp.where(row_ids == col_ids, 1.0, -1.0).astype(F32)
        slopes = -signs * jax.nn.sigmoid(-signs * logits)
    else:
        slopes = jax.nn.sigmoid(logits)
    return slopes.astype(BF)


def image_part_kernel(own, scalars, image_bf, *refs):
    texts, out = refs[:4], refs[4]
    images = image_bf[...]
    total = jnp.zeros(out.shape, F32)
    for k in range(4):
        block = texts[k][...]
        slopes = slopes_of(scalars, images, block, own and k == 0)
        total = total + jnp.dot(slopes, block, preferred_element_type=F32)
    out[...] = (scalars[0] * total).astype(out.dtype)


def proj_grad_kernel(image_unit, image_norm, own, arrived, out):
    unit = image_unit[...]
    total = own[...] + arrived[...].astype(F32)
    along = jnp.sum(unit * total, -1, keepdims=True)
    out[...] = ((total - unit * along) / image_norm[...]).astype(BF)


def text_kernel(scalars, image_own, image_peer, *refs):
    texts, outs = refs[:4], refs[4:]
    own, peer = image_own[...], image_peer[...]
    for k in (1, 2, 3, 0):
        block = texts[k][...]
        part = jnp.dot(slopes_of(scalars, block, own, k == 0), own, preferred_element_type=F32)
        part = part + jnp.dot(
            slopes_of(scalars, block, peer, False), peer, preferred_element_type=F32
        )
        outs[k][...] = (scalars[0] * part).astype(outs[k].dtype)


def local_call(kernel, outs, inputs, scalars=0):
    spaces = [pltpu.SMEM] * scalars + [pltpu.VMEM] * (len(inputs) - scalars)
    results = pl.pallas_call(
        kernel,
        out_shape=[jax.ShapeDtypeStruct(shape, kind) for shape, kind in outs],
        in_specs=[pl.BlockSpec(memory_space=space) for space in spaces],
        out_specs=[pl.BlockSpec(memory_space=pltpu.VMEM)] * len(outs),
        compiler_params=pltpu.CompilerParams(vmem_limit_bytes=VMEM_BYTES),
        cost_estimate=pl.CostEstimate(flops=1, bytes_accessed=1, transcendentals=0),
    )(*inputs)
    return results[0] if len(outs) == 1 else results


def body(image_feats, text_emb, ln_gain, proj_weight, log_temp, bias):
    rows, feat_width = image_feats.shape
    width = proj_weight.shape[1]
    block = (rows, width)

    xl, z, c = (lax.axis_index(name) for name in ("xl", "z", "c"))
    scalars = jnp.stack([jnp.exp(log_temp[0]), bias[0]])
    ids = jnp.stack([lax.axis_index(ROW), c])
    place = weight_row(lax.broadcasted_iota(jnp.int32, (1, feat_width), 1), c, xl, z)
    gains = jnp.pad(in_three(ln_gain), ((0, 13), (0, 0)))
    firsts = [lax.axis_index(axis) & bit == 0 for axis, bit in (("y", 1), ("y", 2), ("c", 1))]
    side = lax.axis_index("xh").reshape(1)
    (image_feats, text_emb, proj_weight), (scalars, ids, place, gains, firsts, side) = (
        lax.optimization_barrier(
            ((image_feats, text_emb, proj_weight), (scalars, ids, place, gains, firsts, side))
        )
    )

    near_z = [moved(proj_weight, "z", by) for by in (1, -1, 2, -2)]
    feats_peer = moved(image_feats, "xh", 1)
    text_bf = local_call(text_unit_kernel, [(block, BF)], [text_emb])

    down_1, up_1, down_2, up_2 = after(near_z, text_bf)
    below = jnp.concatenate([down_1, down_2[:32]])
    above = jnp.concatenate([up_1, up_2[32:]])
    first = jnp.concatenate([proj_weight, down_1, up_1, down_2])
    text_bf, first = after((text_bf, first), below, above)
    below, above = moved(below, "z", 2), moved(above, "z", -2)
    other_first = moved(first, ROW, 1)
    near = around(text_bf, "y")
    second = [up_2, below[:56], above[:56], below[56:], above[56:]]
    second = jnp.concatenate(second)
    second = after(second, below)
    other_second = moved(second, ROW, -1)

    wide = image_feats.shape
    hidden, normed, inv_std, gain, hidden_peer = local_call(
        layer_norm_kernel,
        [(wide, BF), (wide, F32), ((rows, 1), F32), ((1, feat_width), F32), (wide, BF)],
        [place, gains, after(image_feats, second), feats_peer],
    )

    others = after([other_first, other_second], hidden, near)
    weight_mine = jnp.concatenate([first, second] + others)
    weight_other = moved(weight_mine, "c", 1)

    mine, theirs = local_call(
        picked_kernel,
        [((1024, rows), BF)] * 2,
        [ids, place, after(hidden, weight_mine)],
        1,
    )
    theirs = moved(theirs, "c", 1)
    image_bf, image_unit, image_norm, peer_bf = local_call(
        projection_kernel,
        [(block, BF), (block, F32), ((rows, 1), F32), (block, BF)],
        [hidden, hidden_peer, weight_mine, after(weight_other, theirs)],
    )

    texts = [text_bf] + near
    peer_part = local_call(
        functools.partial(image_part_kernel, False), [(block, BF)], [scalars, peer_bf] + texts, 1
    )
    arrived_part = moved(peer_part, "xh", 1)
    text_parts = local_call(
        text_kernel,
        [(block, F32 if k == 0 else BF) for k in range(4)],
        [after(scalars, peer_part), image_bf, peer_bf] + texts,
        1,
    )
    own_part = local_call(
        functools.partial(image_part_kernel, True),
        [(block, F32)],
        [after(scalars, text_parts), image_bf] + texts,
        1,
    )
    proj_grad = local_call(
        proj_grad_kernel, [(block, BF)], [image_unit, image_norm, own_part, arrived_part]
    )
    other_grad = moved(proj_grad, "c", 1)

    mine, theirs = mine.reshape(4, rows, rows), theirs.reshape(4, rows, rows)
    sends = [
        local_call(weight_kernel, [(block, BF)], [mine[k], theirs[k], proj_grad, other_grad])
        for k in (2, 1, 3)
    ]
    arrived = [moved(send, ROW, k) for k, send in zip((2, 1, 3), sends)]

    text_first = after(text_parts[2:], sends)
    text_arrived = [moved(text_first[0], "y", 1), moved(text_first[1], "y", 3)]
    image_grad, gain_part = local_call(
        hidden_grad_kernel,
        [(wide, BF), ((1, feat_width), F32)],
        [place, after(proj_grad, sends), weight_mine, weight_other, normed, inv_std, gain],
    )
    image_grad = local_call(in_order_kernel, [(wide, BF)], [place, image_grad])
    halves = gain_part.reshape(2, feat_width // 2)
    gain_part = jnp.where(firsts[2], halves[0], halves[1])
    gain_part = gain_part + moved(jnp.where(firsts[2], halves[1], halves[0]), "c", 1)
    gain_row = jnp.pad(gain_part, (0, width - feat_width // 2))[None]

    arrived = after(arrived, text_arrived, image_grad)
    total = local_call(
        weight_sum_kernel,
        [(block, BF)],
        [mine[0], theirs[0], proj_grad, other_grad, gain_row] + arrived,
    )
    shared = lax.all_to_all(total.reshape(32, 8, width), ("y", "z"), 0, 0, tiled=True)

    text_arrived.append(moved(after(text_parts[1], total), "y", 2))

    piece = local_call(
        piece_kernel, [((8, width), F32)], [after(shared, text_arrived).reshape(256, width)]
    )
    pieces, gain_part = local_call(
        join_kernel,
        [((16, width), F32), ((1, feat_width // 2), F32)],
        [side, piece, swapped(piece, "xh", 1)],
        1,
    )
    gain_part = gain_part + swapped(gain_part, "xl", 1)
    pieces = both_ways(firsts[0], pieces, swapped(pieces, "y", 1))
    gain_grad = both_ways(firsts[2], gain_part, swapped(gain_part, "c", 1)).reshape(feat_width)
    pieces = after(pieces, gain_part)
    pieces = both_ways(firsts[1], pieces, swapped(pieces, "y", 2))
    pieces = pieces.reshape(4, 2, 8, width).transpose(1, 0, 2, 3)
    weight_grad = pieces[:, :, :7].reshape(56, width)
    text_grad = local_call(
        text_grad_kernel, [(block, BF)], [after(text_emb, piece), text_parts[0]] + text_arrived
    )
    return (image_grad, text_grad, weight_grad, gain_grad)


def solution(mesh):
    fine = Mesh(mesh.devices.reshape(4, 2, 2, 8, 2), AXES)
    whole = P(AXES, None)
    in_specs = (whole, whole, P(), P(FSDP, None), P(), P())
    out_specs = (whole, whole, P(FSDP, None), P())
    return jax.shard_map(body, mesh=fine, in_specs=in_specs, out_specs=out_specs, check_vma=False)
```

```python
import functools

import jax
import jax.numpy as jnp
from jax import lax
from jax.experimental import pallas as pl
from jax.experimental.pallas import tpu as pltpu
from jax.sharding import Mesh, PartitionSpec as P

AXES = ("y", "xh", "xl", "z", "c")
FSDP = ("xl", "z", "c")
ROW = ("xh", "xl")
BF = jnp.bfloat16
F32 = jnp.float32
VMEM_BYTES = 20 * 1024 * 1024
LAST = (((1,), (1,)), ((), ()))


def moved(value, axis, by):
    devices = lax.axis_size(axis)
    return lax.ppermute(value, axis, [(i, (i + by) % devices) for i in range(devices)])


def around(value, axis):
    return [moved(value, axis, -k) for k in (2, 1, 3)]


def after(value, *others):
    return lax.optimization_barrier((value, others))[0]


def swapped(value, axis, bit):
    devices = lax.axis_size(axis)
    return lax.ppermute(value, axis, [(i, i ^ bit) for i in range(devices)])


def both_ways(first, own, other):
    return jnp.where(
        first,
        jnp.concatenate([own, other]),
        jnp.concatenate([other, own]),
    )


def in_three(vector):
    high = lax.reduce_precision(vector, 8, 7)
    middle = lax.reduce_precision(vector - high, 8, 7)
    return jnp.stack([high, middle, vector - high - middle]).astype(BF)


def weight_row(place, core, xl, z):
    core = (core + place // 896) % 2
    xl = (xl + place // 448 % 2) % 2
    block = place // 56 % 8
    away = (block + 1) // 2
    z = (z + jnp.where(block % 2 == 1, 8 - away, away)) % 8
    return (xl * 16 + z * 2 + core) * 56 + place % 56


def text_unit_of(text):
    wide = text[...].astype(F32)
    norm = jnp.sqrt(jnp.sum(wide * wide, -1, keepdims=True) + 1e-06)
    return wide / norm, norm


def text_unit_kernel(text, out):
    out[...] = text_unit_of(text)[0].astype(BF)


def text_grad_kernel(text, own, *refs):
    arrived, out = refs[:-1], refs[-1]
    unit, norm = text_unit_of(text)
    total = own[...]
    for part in arrived:
        total = total + part[...].astype(F32)
    along = jnp.sum(unit * total, -1, keepdims=True)
    out[...] = ((total - unit * along) / norm).astype(BF)


def order_of(place, k):
    rows = lax.broadcasted_iota(jnp.int32, (256, place.shape[1]), 0) + k * 256
    return jnp.where(rows == place, 1.0, 0.0).astype(BF)


def layer_norm_kernel(
    place_ref, gains, feats, feats_peer, hidden, normed, inv_std, gain, hidden_peer
):
    place = place_ref[...]
    gain_parts = jnp.zeros(gains.shape, F32)
    for source in (feats, feats_peer):
        value = jnp.zeros(feats.shape, F32)
        for k in range(feats.shape[1] // 256):
            cut = slice(k * 256, (k + 1) * 256)
            order = order_of(place, k)
            value = value + jnp.dot(source[:, cut], order, preferred_element_type=F32)
            if source is feats:
                gain_parts = gain_parts + jnp.dot(
                    gains[:, cut], order, preferred_element_type=F32
                )
        if source is feats:
            gain[...] = jnp.sum(gain_parts, 0, keepdims=True)
        centered = value - jnp.mean(value, -1, keepdims=True)
        scale = lax.rsqrt(jnp.mean(centered * centered, -1, keepdims=True) + 1e-06)
        value = centered * scale
        if source is feats:
            normed[...] = value
            inv_std[...] = scale
            hidden[...] = (value * gain[...]).astype(BF)
        else:
            hidden_peer[...] = (value * gain[...]).astype(BF)


def picked_kernel(ids, place_ref, hidden, mine, theirs):
    place = place_ref[...]
    index = lax.broadcasted_iota(jnp.int32, (256, 1), 0)
    inside = index & 7
    for k in range(4):
        for core, out in ((ids[1], mine), (1 - ids[1], theirs)):
            to_x = (ids[0] + k) & 3
            shard = (to_x & 1) * 16 + ((index >> 3) & 7) * 2 + core
            found = shard * 56 + (to_x >> 1) * 28 + (index >> 6) * 7 + inside
            found = jnp.where(inside < 7, found, -1)
            choose = jnp.where(found == place, 1.0, 0.0).astype(BF)
            part = lax.dot_general(choose, hidden[...], LAST, preferred_element_type=F32)
            out[k * 256 : (k + 1) * 256] = part.astype(BF)


def projection_kernel(
    hidden, hidden_peer, weight_mine, weight_other, image_bf, image_unit, image_norm, peer_bf
):
    half = weight_mine.shape[0]
    for source in (hidden_peer, hidden):
        projected = jnp.dot(source[:, :half], weight_mine[...], preferred_element_type=F32)
        projected = projected + jnp.dot(
            source[:, half:], weight_other[...], preferred_element_type=F32
        )
        norm = jnp.sqrt(jnp.sum(projected * projected, -1, keepdims=True) + 1e-06)
        unit = projected / norm
        if source is hidden:
            image_norm[...] = norm
            image_unit[...] = unit
            image_bf[...] = unit.astype(BF)
        else:
            peer_bf[...] = unit.astype(BF)


def hidden_grad_kernel(
    place_ref, proj_grad, weight_mine, weight_other, normed_ref, inv_std, gain, out, gain_out
):
    grad = proj_grad[...]
    hidden_grad = jnp.concatenate(
        [
            lax.dot_general(grad, weight[...], LAST, preferred_element_type=F32)
            for weight in (weight_mine, weight_other)
        ],
        1,
    )
    normed = normed_ref[...]
    gain_part = jnp.sum(hidden_grad * normed, 0, keepdims=True)
    high = gain_part.astype(BF)
    gain_part = gain_part - high.astype(F32)
    middle = gain_part.astype(BF)
    low = (gain_part - middle.astype(F32)).astype(BF)
    parts = jnp.concatenate([high, middle, low, jnp.zeros((13, high.shape[1]), BF)])
    place = place_ref[...]
    for k in range(out.shape[1] // 256):
        cut = slice(k * 256, (k + 1) * 256)
        found = lax.dot_general(parts, order_of(place, k), LAST, preferred_element_type=F32)
        gain_out[:, cut] = jnp.sum(found, 0, keepdims=True)
    back = hidden_grad * gain[...]
    out[...] = (
        inv_std[...]
        * (
            back
            - jnp.mean(back, -1, keepdims=True)
            - normed * jnp.mean(back * normed, -1, keepdims=True)
        )
    ).astype(BF)


def in_order_kernel(place_ref, grad, out):
    place = place_ref[...]
    for k in range(out.shape[1] // 256):
        cut = slice(k * 256, (k + 1) * 256)
        order = order_of(place, k)
        out[:, cut] = lax.dot_general(
            grad[...], order, LAST, preferred_element_type=F32
        ).astype(BF)


def weight_kernel(mine, theirs, grad_mine, grad_theirs, out):
    total = jnp.dot(mine[...], grad_mine[...], preferred_element_type=F32)
    total = total + jnp.dot(theirs[...], grad_theirs[...], preferred_element_type=F32)
    out[...] = total.astype(BF)


def weight_sum_kernel(mine, theirs, grad_mine, grad_theirs, gain_row, *refs):
    arrived, out = refs[:-1], refs[-1]
    total = jnp.dot(mine[...], grad_mine[...], preferred_element_type=F32)
    total = total + jnp.dot(theirs[...], grad_theirs[...], preferred_element_type=F32)
    for part in arrived:
        total = total + part[...].astype(F32)
    index = lax.broadcasted_iota(jnp.int32, total.shape, 0)
    out[...] = jnp.where(index & 7 == 7, gain_row[...], total).astype(BF)


def piece_kernel(shared, out):
    total = jnp.zeros(out.shape, F32)
    for k in range(32):
        total = total + shared[k * 8 : (k + 1) * 8].astype(F32)
    out[...] = total


def join_kernel(ids, own, other, pieces, gain_part):
    low = jnp.where(ids[0] == 0, own[...], other[...])
    pieces[:8] = low
    pieces[8:] = jnp.where(ids[0] == 0, other[...], own[...])
    width = gain_part.shape[1]
    gain_part[...] = own[7:, :width] + other[7:, :width]


def slopes_of(scalars, left, right, own):
    dots = lax.dot_general(left, right, LAST, preferred_element_type=F32)
    logits = scalars[0] * dots + scalars[1]
    if own:
        row_ids = lax.broadcasted_iota(jnp.int32, logits.shape, 0)
        col_ids = lax.broadcasted_iota(jnp.int32, logits.shape, 1)
        signs = jnp.where(row_ids == col_ids, 1.0, -1.0).astype(F32)
        slopes = -signs * jax.nn.sigmoid(-signs * logits)
    else:
        slopes = jax.nn.sigmoid(logits)
    return slopes.astype(BF)


def image_part_kernel(own, scalars, image_bf, *refs):
    texts, out = refs[:4], refs[4]
    images = image_bf[...]
    total = jnp.zeros(out.shape, F32)
    for k in range(4):
        block = texts[k][...]
        slopes = slopes_of(scalars, images, block, own and k == 0)
        total = total + jnp.dot(slopes, block, preferred_element_type=F32)
    out[...] = (scalars[0] * total).astype(out.dtype)


def proj_grad_kernel(image_unit, image_norm, own, arrived, out):
    unit = image_unit[...]
    total = own[...] + arrived[...].astype(F32)
    along = jnp.sum(unit * total, -1, keepdims=True)
    out[...] = ((total - unit * along) / image_norm[...]).astype(BF)


def text_kernel(scalars, image_own, image_peer, *refs):
    texts, outs = refs[:4], refs[4:]
    own, peer = image_own[...], image_peer[...]
    for k in (1, 2, 3, 0):
        block = texts[k][...]
        part = jnp.dot(slopes_of(scalars, block, own, k == 0), own, preferred_element_type=F32)
        part = part + jnp.dot(
            slopes_of(scalars, block, peer, False), peer, preferred_element_type=F32
        )
        outs[k][...] = (scalars[0] * part).astype(outs[k].dtype)


def local_call(kernel, outs, inputs, scalars=0):
    spaces = [pltpu.SMEM] * scalars + [pltpu.VMEM] * (len(inputs) - scalars)
    results = pl.pallas_call(
        kernel,
        out_shape=[jax.ShapeDtypeStruct(shape, kind) for shape, kind in outs],
        in_specs=[pl.BlockSpec(memory_space=space) for space in spaces],
        out_specs=[pl.BlockSpec(memory_space=pltpu.VMEM)] * len(outs),
        compiler_params=pltpu.CompilerParams(vmem_limit_bytes=VMEM_BYTES),
        cost_estimate=pl.CostEstimate(flops=1, bytes_accessed=1, transcendentals=0),
    )(*inputs)
    return results[0] if len(outs) == 1 else results


def body(image_feats, text_emb, ln_gain, proj_weight, log_temp, bias):
    rows, feat_width = image_feats.shape
    width = proj_weight.shape[1]
    block = (rows, width)

    xl, z, c = (lax.axis_index(name) for name in ("xl", "z", "c"))
    scalars = jnp.stack([jnp.exp(log_temp[0]), bias[0]])
    ids = jnp.stack([lax.axis_index(ROW), c])
    place = weight_row(lax.broadcasted_iota(jnp.int32, (1, feat_width), 1), c, xl, z)
    gains = jnp.pad(in_three(ln_gain), ((0, 13), (0, 0)))
    firsts = [lax.axis_index(axis) & bit == 0 for axis, bit in (("y", 1), ("y", 2), ("c", 1))]
    side = lax.axis_index("xh").reshape(1)
    (image_feats, text_emb, proj_weight), (scalars, ids, place, gains, firsts, side) = (
        lax.optimization_barrier(
            ((image_feats, text_emb, proj_weight), (scalars, ids, place, gains, firsts, side))
        )
    )

    near_z = [moved(proj_weight, "z", by) for by in (1, -1, 2, -2)]
    feats_peer = moved(image_feats, "xh", 1)
    text_bf = local_call(text_unit_kernel, [(block, BF)], [text_emb])

    down_1, up_1, down_2, up_2 = after(near_z, text_bf)
    below = jnp.concatenate([down_1, down_2[:32]])
    above = jnp.concatenate([up_1, up_2[32:]])
    first = jnp.concatenate([proj_weight, down_1, up_1, down_2])
    text_bf, first = after((text_bf, first), below, above)
    below, above = moved(below, "z", 2), moved(above, "z", -2)
    other_first = moved(first, ROW, 1)
    near = around(text_bf, "y")
    second = [up_2, below[:56], above[:56], below[56:], above[56:]]
    second = jnp.concatenate(second)
    second = after(second, below)
    other_second = moved(second, ROW, -1)

    wide = image_feats.shape
    hidden, normed, inv_std, gain, hidden_peer = local_call(
        layer_norm_kernel,
        [(wide, BF), (wide, F32), ((rows, 1), F32), ((1, feat_width), F32), (wide, BF)],
        [place, gains, after(image_feats, second), feats_peer],
    )

    others = after([other_first, other_second], hidden, near)
    weight_mine = jnp.concatenate([first, second] + others)
    weight_other = moved(weight_mine, "c", 1)

    mine, theirs = local_call(
        picked_kernel,
        [((1024, rows), BF)] * 2,
        [ids, place, after(hidden, weight_mine)],
        1,
    )
    theirs = moved(theirs, "c", 1)
    image_bf, image_unit, image_norm, peer_bf = local_call(
        projection_kernel,
        [(block, BF), (block, F32), ((rows, 1), F32), (block, BF)],
        [hidden, hidden_peer, weight_mine, after(weight_other, theirs)],
    )

    texts = [text_bf] + near
    peer_part = local_call(
        functools.partial(image_part_kernel, False), [(block, BF)], [scalars, peer_bf] + texts, 1
    )
    arrived_part = moved(peer_part, "xh", 1)
    text_parts = local_call(
        text_kernel,
        [(block, F32 if k == 0 else BF) for k in range(4)],
        [after(scalars, peer_part), image_bf, peer_bf] + texts,
        1,
    )
    own_part = local_call(
        functools.partial(image_part_kernel, True),
        [(block, F32)],
        [after(scalars, text_parts), image_bf] + texts,
        1,
    )
    proj_grad = local_call(
        proj_grad_kernel, [(block, BF)], [image_unit, image_norm, own_part, arrived_part]
    )
    other_grad = moved(proj_grad, "c", 1)

    mine, theirs = mine.reshape(4, rows, rows), theirs.reshape(4, rows, rows)
    sends = [
        local_call(weight_kernel, [(block, BF)], [mine[k], theirs[k], proj_grad, other_grad])
        for k in (2, 1, 3)
    ]
    arrived = [moved(send, ROW, k) for k, send in zip((2, 1, 3), sends)]

    text_arrived = [moved(after(text_parts[1], sends), "y", 2)]
    image_grad, gain_part = local_call(
        hidden_grad_kernel,
        [(wide, BF), ((1, feat_width), F32)],
        [place, after(proj_grad, sends), weight_mine, weight_other, normed, inv_std, gain],
    )
    image_grad = local_call(in_order_kernel, [(wide, BF)], [place, image_grad])
    halves = gain_part.reshape(2, feat_width // 2)
    gain_part = jnp.where(firsts[2], halves[0], halves[1])
    gain_part = gain_part + moved(jnp.where(firsts[2], halves[1], halves[0]), "c", 1)
    gain_row = jnp.pad(gain_part, (0, width - feat_width // 2))[None]

    arrived = after(arrived, text_arrived, image_grad)
    total = local_call(
        weight_sum_kernel,
        [(block, BF)],
        [mine[0], theirs[0], proj_grad, other_grad, gain_row] + arrived,
    )
    shared = lax.all_to_all(total.reshape(32, 8, width), ("y", "z"), 0, 0, tiled=True)

    text_ends = after(text_parts[2:], total)
    text_arrived += [moved(text_ends[0], "y", 1), moved(text_ends[1], "y", 3)]

    piece = local_call(
        piece_kernel, [((8, width), F32)], [after(shared, text_arrived).reshape(256, width)]
    )
    pieces, gain_part = local_call(
        join_kernel,
        [((16, width), F32), ((1, feat_width // 2), F32)],
        [side, piece, swapped(piece, "xh", 1)],
        1,
    )
    gain_part = gain_part + swapped(gain_part, "xl", 1)
    pieces = both_ways(firsts[0], pieces, swapped(pieces, "y", 1))
    gain_grad = both_ways(firsts[2], gain_part, swapped(gain_part, "c", 1)).reshape(feat_width)
    pieces = after(pieces, gain_part)
    pieces = both_ways(firsts[1], pieces, swapped(pieces, "y", 2))
    pieces = pieces.reshape(4, 2, 8, width).transpose(1, 0, 2, 3)
    weight_grad = pieces[:, :, :7].reshape(56, width)
    text_grad = local_call(
        text_grad_kernel, [(block, BF)], [after(text_emb, piece), text_parts[0]] + text_arrived
    )
    return (image_grad, text_grad, weight_grad, gain_grad)


def solution(mesh):
    fine = Mesh(mesh.devices.reshape(4, 2, 2, 8, 2), AXES)
    whole = P(AXES, None)
    in_specs = (whole, whole, P(), P(FSDP, None), P(), P())
    out_specs = (whole, whole, P(FSDP, None), P())
    return jax.shard_map(body, mesh=fine, in_specs=in_specs, out_specs=out_specs, check_vma=False)
```

```python
import functools

import jax
import jax.numpy as jnp
from jax import lax
from jax.experimental import pallas as pl
from jax.experimental.pallas import tpu as pltpu
from jax.sharding import Mesh, PartitionSpec as P

AXES = ("y", "xh", "xl", "z", "c")
FSDP = ("xl", "z", "c")
ROW = ("xh", "xl")
BF = jnp.bfloat16
F32 = jnp.float32
VMEM_BYTES = 20 * 1024 * 1024
LAST = (((1,), (1,)), ((), ()))


def moved(value, axis, by):
    devices = lax.axis_size(axis)
    return lax.ppermute(value, axis, [(i, (i + by) % devices) for i in range(devices)])


def around(value, axis):
    return [moved(value, axis, -k) for k in (2, 1, 3)]


def after(value, *others):
    return lax.optimization_barrier((value, others))[0]


def swapped(value, axis, bit):
    devices = lax.axis_size(axis)
    return lax.ppermute(value, axis, [(i, i ^ bit) for i in range(devices)])


def both_ways(first, own, other):
    return jnp.where(
        first,
        jnp.concatenate([own, other]),
        jnp.concatenate([other, own]),
    )


def in_three(vector):
    high = lax.reduce_precision(vector, 8, 7)
    middle = lax.reduce_precision(vector - high, 8, 7)
    return jnp.stack([high, middle, vector - high - middle]).astype(BF)


def weight_row(place, core, xl, z):
    core = (core + place // 896) % 2
    xl = (xl + place // 448 % 2) % 2
    block = place // 56 % 8
    away = (block + 1) // 2
    z = (z + jnp.where(block % 2 == 1, 8 - away, away)) % 8
    return (xl * 16 + z * 2 + core) * 56 + place % 56


def text_unit_of(text):
    wide = text[...].astype(F32)
    norm = jnp.sqrt(jnp.sum(wide * wide, -1, keepdims=True) + 1e-06)
    return wide / norm, norm


def text_unit_kernel(text, out):
    out[...] = text_unit_of(text)[0].astype(BF)


def text_grad_kernel(text, own, *refs):
    arrived, out = refs[:-1], refs[-1]
    unit, norm = text_unit_of(text)
    total = own[...]
    for part in arrived:
        total = total + part[...].astype(F32)
    along = jnp.sum(unit * total, -1, keepdims=True)
    out[...] = ((total - unit * along) / norm).astype(BF)


def order_of(place, k):
    rows = lax.broadcasted_iota(jnp.int32, (256, place.shape[1]), 0) + k * 256
    return jnp.where(rows == place, 1.0, 0.0).astype(BF)


def layer_norm_kernel(
    place_ref, gains, feats, feats_peer, hidden, normed, inv_std, gain, hidden_peer
):
    place = place_ref[...]
    gain_parts = jnp.zeros(gains.shape, F32)
    for source in (feats, feats_peer):
        value = jnp.zeros(feats.shape, F32)
        for k in range(feats.shape[1] // 256):
            cut = slice(k * 256, (k + 1) * 256)
            order = order_of(place, k)
            value = value + jnp.dot(source[:, cut], order, preferred_element_type=F32)
            if source is feats:
                gain_parts = gain_parts + jnp.dot(
                    gains[:, cut], order, preferred_element_type=F32
                )
        if source is feats:
            gain[...] = jnp.sum(gain_parts, 0, keepdims=True)
        centered = value - jnp.mean(value, -1, keepdims=True)
        scale = lax.rsqrt(jnp.mean(centered * centered, -1, keepdims=True) + 1e-06)
        value = centered * scale
        if source is feats:
            normed[...] = value
            inv_std[...] = scale
            hidden[...] = (value * gain[...]).astype(BF)
        else:
            hidden_peer[...] = (value * gain[...]).astype(BF)


def picked_kernel(ids, place_ref, hidden, mine, theirs):
    place = place_ref[...]
    index = lax.broadcasted_iota(jnp.int32, (256, 1), 0)
    inside = index & 7
    for k in range(4):
        for core, out in ((ids[1], mine), (1 - ids[1], theirs)):
            to_x = (ids[0] + k) & 3
            shard = (to_x & 1) * 16 + ((index >> 3) & 7) * 2 + core
            found = shard * 56 + (to_x >> 1) * 28 + (index >> 6) * 7 + inside
            found = jnp.where(inside < 7, found, -1)
            choose = jnp.where(found == place, 1.0, 0.0).astype(BF)
            part = lax.dot_general(choose, hidden[...], LAST, preferred_element_type=F32)
            out[k * 256 : (k + 1) * 256] = part.astype(BF)


def projection_kernel(
    hidden, hidden_peer, weight_mine, weight_other, image_bf, image_unit, image_norm, peer_bf
):
    half = weight_mine.shape[0]
    for source in (hidden_peer, hidden):
        projected = jnp.dot(source[:, :half], weight_mine[...], preferred_element_type=F32)
        projected = projected + jnp.dot(
            source[:, half:], weight_other[...], preferred_element_type=F32
        )
        norm = jnp.sqrt(jnp.sum(projected * projected, -1, keepdims=True) + 1e-06)
        unit = projected / norm
        if source is hidden:
            image_norm[...] = norm
            image_unit[...] = unit
            image_bf[...] = unit.astype(BF)
        else:
            peer_bf[...] = unit.astype(BF)


def hidden_grad_kernel(
    place_ref, proj_grad, weight_mine, weight_other, normed_ref, inv_std, gain, out, gain_out
):
    grad = proj_grad[...]
    hidden_grad = jnp.concatenate(
        [
            lax.dot_general(grad, weight[...], LAST, preferred_element_type=F32)
            for weight in (weight_mine, weight_other)
        ],
        1,
    )
    normed = normed_ref[...]
    gain_part = jnp.sum(hidden_grad * normed, 0, keepdims=True)
    high = gain_part.astype(BF)
    gain_part = gain_part - high.astype(F32)
    middle = gain_part.astype(BF)
    low = (gain_part - middle.astype(F32)).astype(BF)
    parts = jnp.concatenate([high, middle, low, jnp.zeros((13, high.shape[1]), BF)])
    place = place_ref[...]
    for k in range(out.shape[1] // 256):
        cut = slice(k * 256, (k + 1) * 256)
        found = lax.dot_general(parts, order_of(place, k), LAST, preferred_element_type=F32)
        gain_out[:, cut] = jnp.sum(found, 0, keepdims=True)
    back = hidden_grad * gain[...]
    out[...] = (
        inv_std[...]
        * (
            back
            - jnp.mean(back, -1, keepdims=True)
            - normed * jnp.mean(back * normed, -1, keepdims=True)
        )
    ).astype(BF)


def in_order_kernel(place_ref, grad, out):
    place = place_ref[...]
    for k in range(out.shape[1] // 256):
        cut = slice(k * 256, (k + 1) * 256)
        order = order_of(place, k)
        out[:, cut] = lax.dot_general(
            grad[...], order, LAST, preferred_element_type=F32
        ).astype(BF)


def weight_kernel(mine, theirs, grad_mine, grad_theirs, out):
    total = jnp.dot(mine[...], grad_mine[...], preferred_element_type=F32)
    total = total + jnp.dot(theirs[...], grad_theirs[...], preferred_element_type=F32)
    out[...] = total.astype(BF)


def weight_sum_kernel(mine, theirs, grad_mine, grad_theirs, gain_row, *refs):
    arrived, out = refs[:-1], refs[-1]
    total = jnp.dot(mine[...], grad_mine[...], preferred_element_type=F32)
    total = total + jnp.dot(theirs[...], grad_theirs[...], preferred_element_type=F32)
    for part in arrived:
        total = total + part[...].astype(F32)
    index = lax.broadcasted_iota(jnp.int32, total.shape, 0)
    out[...] = jnp.where(index & 7 == 7, gain_row[...], total).astype(BF)


def piece_kernel(shared, out):
    total = jnp.zeros(out.shape, F32)
    for k in range(32):
        total = total + shared[k * 8 : (k + 1) * 8].astype(F32)
    out[...] = total


def join_kernel(ids, own, other, pieces, gain_part):
    low = jnp.where(ids[0] == 0, own[...], other[...])
    pieces[:8] = low
    pieces[8:] = jnp.where(ids[0] == 0, other[...], own[...])
    width = gain_part.shape[1]
    gain_part[...] = own[7:, :width] + other[7:, :width]


def slopes_of(scalars, left, right, own):
    dots = lax.dot_general(left, right, LAST, preferred_element_type=F32)
    logits = scalars[0] * dots + scalars[1]
    if own:
        row_ids = lax.broadcasted_iota(jnp.int32, logits.shape, 0)
        col_ids = lax.broadcasted_iota(jnp.int32, logits.shape, 1)
        signs = jnp.where(row_ids == col_ids, 1.0, -1.0).astype(F32)
        slopes = -signs * jax.nn.sigmoid(-signs * logits)
    else:
        slopes = jax.nn.sigmoid(logits)
    return slopes.astype(BF)


def image_part_kernel(own, scalars, image_bf, *refs):
    texts, out = refs[:4], refs[4]
    images = image_bf[...]
    total = jnp.zeros(out.shape, F32)
    for k in range(4):
        block = texts[k][...]
        slopes = slopes_of(scalars, images, block, own and k == 0)
        total = total + jnp.dot(slopes, block, preferred_element_type=F32)
    out[...] = (scalars[0] * total).astype(out.dtype)


def proj_grad_kernel(image_unit, image_norm, own, arrived, out):
    unit = image_unit[...]
    total = own[...] + arrived[...].astype(F32)
    along = jnp.sum(unit * total, -1, keepdims=True)
    out[...] = ((total - unit * along) / image_norm[...]).astype(BF)


def text_kernel(scalars, image_own, image_peer, *refs):
    texts, outs = refs[:4], refs[4:]
    own, peer = image_own[...], image_peer[...]
    for k in (1, 2, 3, 0):
        block = texts[k][...]
        part = jnp.dot(slopes_of(scalars, block, own, k == 0), own, preferred_element_type=F32)
        part = part + jnp.dot(
            slopes_of(scalars, block, peer, False), peer, preferred_element_type=F32
        )
        outs[k][...] = (scalars[0] * part).astype(outs[k].dtype)


def local_call(kernel, outs, inputs, scalars=0):
    spaces = [pltpu.SMEM] * scalars + [pltpu.VMEM] * (len(inputs) - scalars)
    results = pl.pallas_call(
        kernel,
        out_shape=[jax.ShapeDtypeStruct(shape, kind) for shape, kind in outs],
        in_specs=[pl.BlockSpec(memory_space=space) for space in spaces],
        out_specs=[pl.BlockSpec(memory_space=pltpu.VMEM)] * len(outs),
        compiler_params=pltpu.CompilerParams(vmem_limit_bytes=VMEM_BYTES),
        cost_estimate=pl.CostEstimate(flops=1, bytes_accessed=1, transcendentals=0),
    )(*inputs)
    return results[0] if len(outs) == 1 else results


def body(image_feats, text_emb, ln_gain, proj_weight, log_temp, bias):
    rows, feat_width = image_feats.shape
    width = proj_weight.shape[1]
    block = (rows, width)

    xl, z, c = (lax.axis_index(name) for name in ("xl", "z", "c"))
    scalars = jnp.stack([jnp.exp(log_temp[0]), bias[0]])
    ids = jnp.stack([lax.axis_index(ROW), c])
    place = weight_row(lax.broadcasted_iota(jnp.int32, (1, feat_width), 1), c, xl, z)
    gains = jnp.pad(in_three(ln_gain), ((0, 13), (0, 0)))
    firsts = [lax.axis_index(axis) & bit == 0 for axis, bit in (("y", 1), ("y", 2), ("c", 1))]
    side = lax.axis_index("xh").reshape(1)
    (image_feats, text_emb, proj_weight), (scalars, ids, place, gains, firsts, side) = (
        lax.optimization_barrier(
            ((image_feats, text_emb, proj_weight), (scalars, ids, place, gains, firsts, side))
        )
    )

    near_z = [moved(proj_weight, "z", by) for by in (1, -1, 2, -2)]
    feats_peer = moved(image_feats, "xh", 1)
    text_bf = local_call(text_unit_kernel, [(block, BF)], [text_emb])

    down_1, up_1, down_2, up_2 = after(near_z, text_bf)
    below = jnp.concatenate([down_1, down_2[:32]])
    above = jnp.concatenate([up_1, up_2[32:]])
    first = jnp.concatenate([proj_weight, down_1, up_1, down_2])
    text_bf, first = after((text_bf, first), below, above)
    below, above = moved(below, "z", 2), moved(above, "z", -2)
    other_first = moved(first, ROW, 1)
    near = around(text_bf, "y")
    second = [up_2, below[:56], above[:56], below[56:], above[56:]]
    second = jnp.concatenate(second)
    second = after(second, below)
    other_second = moved(second, ROW, -1)

    wide = image_feats.shape
    hidden, normed, inv_std, gain, hidden_peer = local_call(
        layer_norm_kernel,
        [(wide, BF), (wide, F32), ((rows, 1), F32), ((1, feat_width), F32), (wide, BF)],
        [place, gains, after(image_feats, second), feats_peer],
    )

    others = after([other_first, other_second], hidden, near)
    weight_mine = jnp.concatenate([first, second] + others)
    weight_other = moved(weight_mine, "c", 1)

    mine, theirs = local_call(
        picked_kernel,
        [((1024, rows), BF)] * 2,
        [ids, place, after(hidden, weight_mine)],
        1,
    )
    theirs = moved(theirs, "c", 1)
    image_bf, image_unit, image_norm, peer_bf = local_call(
        projection_kernel,
        [(block, BF), (block, F32), ((rows, 1), F32), (block, BF)],
        [hidden, hidden_peer, weight_mine, after(weight_other, theirs)],
    )

    texts = [text_bf] + near
    peer_part = local_call(
        functools.partial(image_part_kernel, False), [(block, BF)], [scalars, peer_bf] + texts, 1
    )
    arrived_part = moved(peer_part, "xh", 1)
    text_parts = local_call(
        text_kernel,
        [(block, F32 if k == 0 else BF) for k in range(4)],
        [after(scalars, peer_part), image_bf, peer_bf] + texts,
        1,
    )
    own_part = local_call(
        functools.partial(image_part_kernel, True),
        [(block, F32)],
        [after(scalars, text_parts), image_bf] + texts,
        1,
    )
    proj_grad = local_call(
        proj_grad_kernel, [(block, BF)], [image_unit, image_norm, own_part, arrived_part]
    )
    other_grad = moved(proj_grad, "c", 1)

    mine, theirs = mine.reshape(4, rows, rows), theirs.reshape(4, rows, rows)
    sends = [
        local_call(weight_kernel, [(block, BF)], [mine[k], theirs[k], proj_grad, other_grad])
        for k in (2, 1, 3)
    ]
    arrived = [moved(send, ROW, k) for k, send in zip((2, 1, 3), sends)]

    text_arrived = [moved(after(text_parts[1], sends), "y", 2)]
    text_arrived.append(moved(after(text_parts[2], text_arrived[0]), "y", 1))
    image_grad, gain_part = local_call(
        hidden_grad_kernel,
        [(wide, BF), ((1, feat_width), F32)],
        [place, after(proj_grad, sends), weight_mine, weight_other, normed, inv_std, gain],
    )
    image_grad = local_call(in_order_kernel, [(wide, BF)], [place, image_grad])
    halves = gain_part.reshape(2, feat_width // 2)
    gain_part = jnp.where(firsts[2], halves[0], halves[1])
    gain_part = gain_part + moved(jnp.where(firsts[2], halves[1], halves[0]), "c", 1)
    gain_row = jnp.pad(gain_part, (0, width - feat_width // 2))[None]

    arrived = after(arrived, text_arrived, image_grad)
    total = local_call(
        weight_sum_kernel,
        [(block, BF)],
        [mine[0], theirs[0], proj_grad, other_grad, gain_row] + arrived,
    )
    shared = lax.all_to_all(total.reshape(32, 8, width), ("y", "z"), 0, 0, tiled=True)

    text_arrived.append(moved(after(text_parts[3], total), "y", 3))

    piece = local_call(
        piece_kernel, [((8, width), F32)], [after(shared, text_arrived).reshape(256, width)]
    )
    pieces, gain_part = local_call(
        join_kernel,
        [((16, width), F32), ((1, feat_width // 2), F32)],
        [side, piece, swapped(piece, "xh", 1)],
        1,
    )
    gain_part = gain_part + swapped(gain_part, "xl", 1)
    pieces = both_ways(firsts[0], pieces, swapped(pieces, "y", 1))
    gain_grad = both_ways(firsts[2], gain_part, swapped(gain_part, "c", 1)).reshape(feat_width)
    pieces = after(pieces, gain_part)
    pieces = both_ways(firsts[1], pieces, swapped(pieces, "y", 2))
    pieces = pieces.reshape(4, 2, 8, width).transpose(1, 0, 2, 3)
    weight_grad = pieces[:, :, :7].reshape(56, width)
    text_grad = local_call(
        text_grad_kernel, [(block, BF)], [after(text_emb, piece), text_parts[0]] + text_arrived
    )
    return (image_grad, text_grad, weight_grad, gain_grad)


def solution(mesh):
    fine = Mesh(mesh.devices.reshape(4, 2, 2, 8, 2), AXES)
    whole = P(AXES, None)
    in_specs = (whole, whole, P(), P(FSDP, None), P(), P())
    out_specs = (whole, whole, P(FSDP, None), P())
    return jax.shard_map(body, mesh=fine, in_specs=in_specs, out_specs=out_specs, check_vma=False)
```
